32 devices in a mesh: gx: 2 (over core), gy: 4 (over z), gz: 4 (over y, x).
Axes of the slice: x: 2, y: 2, z: 4, core: 2. Of those that a mesh axis runs over, the one named last changes fastest.
Arguments:
- cr_init: float32 [64, 16, 8, 512], P(None, 'gz', 'gx', 'gy'), may hold values from 0.1 to 3
- gas: float32 [16, 8, 512], P('gz', 'gx', 'gy'), may hold values from 0.05 to 3
- diff_coeff: float32 [64], replicated, may hold values from 0.06 to 0.14
- loss_coeff: float32 [64], replicated, may hold values from 0.05 to 0.3
- pi0_table: float32 [96, 64], replicated, may hold values from -0.75 to 0.75
- los_weight: bfloat16 [4, 2, 4, 7, 2048, 128], P('gz', 'gx', 'gy'), may hold values from -0.125 to 0.125
- slot_owner: int32 [4, 2, 4, 7, 1], P('gz', 'gx', 'gy'), may hold values from 0 to 3; in each aligned block of 7 rows (0 to 6, 7 to 13, ..., all dimensions but the last counted through in order) at most 3 rows name the same one
- slot_block: int32 [4, 2, 4, 7], P('gz', 'gx', 'gy'), may hold values from 0 to 3
Outputs:
- cr_final: float32 [64, 16, 8, 512], P(None, 'gz', 'gx', 'gy')
- sky: float32 [4, 2, 16, 96, 128], P('gz', 'gx', 'gy')
The draws below stay inside these ranges and needn't reach their ends.
Inputs may be any that keep to these rules, and one draw needn't show every extreme that they name: `slot_owner`: at most 3 of the 7 weight blocks of one device name the same owner, and some device names one owner exactly 3 times.
All inputs are finite; a program needn't handle non-finite values.
Results may differ from the reference program's by a relative error of at most 0.0029.
Values sent between devices are 32-bit elements; how exact they have to be, the bound alone decides.
A program may use at most 64 MiB of HBM per device.

```python
import math
import jax
import jax.numpy as jnp
import numpy as np
from jax import lax

NE = 64
NG = 96
PB = 128
CX = 4
CY = 128
CZ = 4
STEPS = 2
KS = 7
BO = 4
CAP = 3
CELLS = 2048
NX = 8
NY = 512
NZ = 16
N_GX = 2
N_GY = 4
N_GZ = 4


def draw_cr_init(key, part):
    key_base = jax.random.fold_in(key, 11)
    key_high = jax.random.fold_in(key, 12)
    shape = (NE, NZ, NX, NY)
    base = jnp.exp(jax.random.uniform(key_base, shape, jnp.float32, math.log(0.1), math.log(0.3)))
    high = jnp.exp(jax.random.uniform(key_high, shape, jnp.float32, math.log(1.0), math.log(3.0)))
    place = jnp.arange(NY) % CY
    second = (place == 1) | (place == CY - 2)
    return jnp.where(second[None, None, None, :], high, base).astype(jnp.float32)


def draw_gas(key, part):
    key_base = jax.random.fold_in(key, 21)
    key_face = jax.random.fold_in(key, 22)
    shape = (NZ, NX, NY)
    base = jnp.exp(jax.random.uniform(key_base, shape, jnp.float32, math.log(0.05), math.log(0.15)))
    face = jnp.exp(jax.random.uniform(key_face, shape, jnp.float32, math.log(1.0), math.log(3.0)))
    place = jnp.arange(NY) % CY
    outer = (place == 0) | (place == CY - 1)
    return jnp.where(outer[None, None, :], face, base).astype(jnp.float32)


def plant(entries, rng, smallest, largest):
    longest = entries.shape.index(max(entries.shape))
    spots = []
    for shift in (0, 1):
        where = [jax.random.randint(jax.random.fold_in(rng, axis), (), 0, length) for axis, length in enumerate(entries.shape)]
        where[longest] = (where[longest] + shift) % entries.shape[longest]
        spots.append(tuple(where))
    return entries.at[spots[0]].set(smallest).at[spots[1]].set(largest)


def steps_of(key, dims, cuts, low, high):
    gain = 1.0
    for position, parts in cuts:
        draws = jax.random.uniform(jax.random.fold_in(jax.random.fold_in(key, 6), position), (parts,), jnp.float32, low / len(cuts), high / len(cuts))
        gain = gain * jnp.repeat(jnp.exp(draws), dims[position] // parts).reshape((-1,) + (1,) * (len(dims) - 1 - position))
    return gain


def shared_out(own_key, own, number, rows, amount, top, bound, skew):
    sequence = jax.random.permutation(own_key, amount)
    crowded, common = portions_of(amount, rows * top, bound, skew, True), portions_of(amount, rows * top, bound, skew, False)
    places = jnp.arange(amount)

    def named(sizes, offset_by):
        used = int((sizes > 0).sum())
        fixed = max(1, used // 4)
        moved = fixed + (places - fixed + offset_by * (used - fixed)) % max(1, amount - fixed)
        return jnp.zeros((amount,), jnp.int32).at[sequence[jnp.where(places < fixed, places, moved)]].set(jnp.asarray(sizes, jnp.int32))

    sizes = jnp.where(number % 4 == 0, named(crowded, number // 4), named(common, number - number // 4 - 1))
    mixed = jax.random.permutation(jax.random.fold_in(own, 3), amount)
    source_of, taker = mixed[0:amount // 2 * 2:2], mixed[1:amount // 2 * 2:2]
    room = jnp.minimum(sizes[source_of] - 1, bound - sizes[taker]) // 2
    room = jnp.where((source_of == sequence[0]) | (taker == sequence[0]) | (sizes[taker] == 0), 0, jnp.maximum(room, 0))
    moved = jax.random.randint(jax.random.fold_in(own, 4), (amount // 2,), 0, 1 << 20) % (room + 1)
    sizes = sizes.at[source_of].add(-moved).at[taker].add(moved)
    labels = jnp.searchsorted(jnp.cumsum(sizes), jnp.arange(rows * top), side="right").astype(jnp.int32)
    grid = labels.reshape(top, rows).T
    grid = grid[jax.random.permutation(jax.random.fold_in(own, 1), rows)]
    offset_by = jax.random.randint(jax.random.fold_in(own, 2), (rows, 1), 0, top)
    return jnp.take_along_axis(grid, (jnp.arange(top)[None, :] + offset_by) % top, axis=1)


def portions_of(count, total, limit, skew, full):
    portions = [(1 << 20) // math.isqrt(grade ** skew) + 1 for grade in range(1, count + 1)]
    largest = limit if full else min(limit, max(-(-total // count), total * portions[0] // sum(portions)))
    least = 1 if total - largest >= count - 1 else 0
    holding, spare = [largest] + [least] * (count - 1), total - largest - least * (count - 1)
    while spare > 0:
        free = [i for i in range(1, count) if holding[i] < largest] or [i for i in range(1, count) if holding[i] < limit]
        pool, left = sum([portions[i] for i in free]), spare
        for i in free:
            more = min(limit - holding[i], max(1, left * portions[i] // pool), spare)
            holding[i] = holding[i] + more
            spare = spare - more
    return np.array(holding)


def normal_values(rng, extent, scale, most, split=(), dtype=jnp.bfloat16):
    array = scale * jax.random.normal(rng, extent, jnp.float32)
    if split:
        array = array * steps_of(rng, extent, split, -0.22, 0.18)
    return jnp.clip(array, -most, most).astype(dtype)


def setup_inputs(seed: int = 0) -> dict:
    key_list = jax.random.split(jax.random.key(seed), 9)
    cr_init = draw_cr_init(jax.random.fold_in(key_list[8], 71), 0)
    gas = draw_gas(jax.random.fold_in(key_list[8], 71), 0)
    diff_coeff = jnp.clip(jax.random.uniform(key_list[2], (NE,), jnp.float32, 0.06, 0.14), 0.06, 0.14)
    loss_coeff = jnp.clip(jnp.exp(jax.random.uniform(key_list[3], (NE,), jnp.float32, math.log(0.05), math.log(0.3))), 0.05, 0.3)
    pi0_table = normal_values(key_list[4], (NG, NE), NE ** -0.5, 0.75, (), jnp.float32)
    los_weight = normal_values(key_list[5], (N_GZ, N_GX, N_GY, KS, CELLS, PB), CELLS ** -0.5, 0.125, ((0, 4), (1, 2), (2, 4)))
    slot_owner_keys = jax.random.split(jax.random.fold_in(key_list[6], 1), N_GZ * N_GX * N_GY * KS // KS)
    slot_owner_turns = jax.random.permutation(jax.random.fold_in(key_list[6], 3), N_GZ * N_GX * N_GY * KS // KS)
    slot_owner = jax.vmap(lambda own, number: shared_out(jax.random.fold_in(key_list[6], 2), own, number, KS, N_GY, 1, CAP, 2))(slot_owner_keys, slot_owner_turns).reshape((N_GZ, N_GX, N_GY, KS, 1))
    slot_block = plant(jax.random.randint(key_list[7], (N_GZ, N_GX, N_GY, KS), 0, BO), jax.random.fold_in(key_list[7], 1), 0, BO - 1).astype(jnp.int32)
    return {"cr_init": cr_init, "gas": gas, "diff_coeff": diff_coeff, "loss_coeff": loss_coeff, "pi0_table": pi0_table, "los_weight": los_weight, "slot_owner": slot_owner, "slot_block": slot_block}


def advance(padded, diffusion, losses):
    center = padded[:, 1:-1, 1:-1, 1:-1]
    beside = padded[:, 2:, 1:-1, 1:-1] + padded[:, :-2, 1:-1, 1:-1]
    beside = beside + padded[:, 1:-1, 2:, 1:-1] + padded[:, 1:-1, :-2, 1:-1]
    beside = beside + padded[:, 1:-1, 1:-1, 2:] + padded[:, 1:-1, 1:-1, :-2]
    loss_flux = losses[:, None, None, None] * center
    from_above = jnp.concatenate([loss_flux[1:], jnp.zeros_like(loss_flux[:1])], axis=0)
    return center + diffusion[:, None, None, None] * (beside - 6.0 * center) + from_above - loss_flux


def reference(cr_init, gas, diff_coeff, loss_coeff, pi0_table, los_weight, slot_owner, slot_block):
    density = cr_init
    for step_index in range(STEPS):
        padded = jnp.pad(density, ((0, 0), (1, 1), (1, 1), (1, 1)))
        density = advance(padded, diff_coeff, loss_coeff)
    source = jnp.einsum("ge,ezxy->gzxy", pi0_table, density, precision=lax.Precision.HIGHEST)
    emissivity = (gas[None] * source).astype(jnp.bfloat16)
    tile_rows = emissivity.reshape(NG, N_GZ, CZ, N_GX, CX, N_GY, CY)
    tile_rows = tile_rows.transpose(1, 3, 5, 0, 2, 4, 6).reshape(N_GZ * N_GX, N_GY, NG, CELLS)
    weights = los_weight.reshape(N_GZ * N_GX, N_GY, KS, CELLS, PB)
    owners = slot_owner.reshape(N_GZ * N_GX, N_GY, KS).astype(jnp.int32)
    blocks = slot_block.reshape(N_GZ * N_GX, N_GY, KS).astype(jnp.int32)

    def project(operands):
        row_tiles, row_weights, row_owners, row_blocks = operands
        contrib = jnp.einsum("jgc,jscp->jsgp", row_tiles.astype(jnp.float32), row_weights.astype(jnp.float32), precision=lax.Precision.HIGHEST)
        target = (row_owners * BO + row_blocks).reshape(-1).astype(jnp.int32)
        return jax.ops.segment_sum(contrib.reshape(N_GY * KS, NG, PB), target, num_segments=N_GY * BO)

    sky = lax.map(project, (tile_rows, weights, owners, blocks))
    return density, sky.reshape(N_GZ, N_GX, N_GY * BO, NG, PB)
```

```python
import functools

import jax
import jax.numpy as jnp
from jax import lax
from jax.experimental import pallas as pl
from jax.experimental.pallas import tpu as pltpu
from jax.sharding import PartitionSpec as P

BO = 4
CAP = 3
CHUNKS = 4
PAD = 8
MESH = pl.DeviceIdType.MESH


def kernel(
    sizes, cr_ref, gas_ref, diff_ref, loss_ref, pi0_ref, owner_ref, block_ref, weight_hbm,
    out_ref, sky_ref,
    first, second, halo_z, halo_x, halo_y, pack, coef, weights, lhs, contrib, slots, landed,
    names, landed_names,
    weight_sem, halo_send, halo_recv, sky_send, sky_recv, name_send, name_recv,
):
    nx, ny, nz = sizes
    energies = diff_ref.shape[1]
    cz, cx = first.shape[0], first.shape[1]
    lanes = first.shape[3]
    cells = cz * cx
    size = energies // CHUNKS
    slot_count = weights.shape[0]
    gx, gy, gz = lax.axis_index("gx"), lax.axis_index("gy"), lax.axis_index("gz")

    load = pltpu.make_async_copy(weight_hbm, weights, weight_sem)
    load.start()

    exists = (gz > 0, gz < nz - 1, gx > 0, gx < nx - 1, gy > 0, gy < ny - 1)
    places = (
        (gx, gy, gz - 1), (gx, gy, gz + 1), (gx - 1, gy, gz), (gx + 1, gy, gz),
        (gx, gy - 1, gz), (gx, gy + 1, gz),
    )

    barrier = pltpu.get_barrier_semaphore()
    for side in range(4):
        @pl.when(exists[side])
        def _(side=side):
            pl.semaphore_signal(barrier, inc=1, device_id=places[side], device_id_type=MESH)
    for offset in range(1, ny):
        pl.semaphore_signal(
            barrier, inc=1, device_id=(gx, lax.rem(gy + offset, ny), gz), device_id_type=MESH
        )

    for cell in range(cells):
        first[cell // cx, cell % cx, 0:energies, :] = cr_ref[pl.ds(cell, energies, stride=cells), :]
    first[:, :, energies:, :] = jnp.zeros((cz, cx, PAD, lanes), jnp.float32)
    second[:, :, energies:, :] = jnp.zeros((cz, cx, PAD, lanes), jnp.float32)

    row = lax.broadcasted_iota(jnp.int32, (energies, energies), 0)
    column = lax.broadcasted_iota(jnp.int32, (energies, energies), 1)
    diff = jnp.broadcast_to(diff_ref[...], (energies, energies))
    loss = jnp.broadcast_to(loss_ref[...], (energies, energies))
    for index, (values, mask) in enumerate(
        ((diff, row == column), (loss, row == column), (loss, row + 1 == column))
    ):
        spread = jnp.sum(jnp.where(mask, values, 0.0), axis=1, keepdims=True)
        coef[index] = jnp.broadcast_to(spread, (energies, lanes))

    for side in range(6):
        @pl.when(jnp.logical_not(exists[side]))
        def _(side=side):
            halo = (halo_z, halo_x, halo_y)[side // 2]
            for step in range(2):
                halo[step, side % 2] = jnp.zeros(halo.shape[2:], jnp.float32)

    lane = lax.broadcasted_iota(jnp.int32, (size, lanes), 1)
    rows_of = [pl.ds(energies - size * (c + 1), size) for c in range(CHUNKS)]

    def halo_copy(step, chunk, side, arriving):
        rows = rows_of[chunk]
        source = (first, second)[step]
        far = side % 2 == 1
        if side < 2:
            src = source.at[cz - 1 if far else 0, :, rows, :]
        elif side < 4:
            src = source.at[:, cx - 1 if far else 0, rows, :]
        else:
            src = pack.at[step, rows, :]
        halo = (halo_z, halo_x, halo_y)[side // 2]
        lands = side % 2 if arriving else 1 - side % 2
        sem_side = side if arriving else side ^ 1
        if side < 4:
            dst = halo.at[step, lands, :, rows, :]
        else:
            dst = halo.at[step, lands, rows, :]
        return pltpu.make_async_remote_copy(
            src_ref=src, dst_ref=dst,
            send_sem=halo_send.at[step, chunk, side],
            recv_sem=halo_recv.at[step, chunk, sem_side],
            device_id=places[side], device_id_type=MESH,
        )

    def pack_rows(step, chunk):
        source = (first, second)[step]
        packed = jnp.zeros((size, lanes), jnp.float32)
        for cell in range(cells):
            turned = pltpu.roll(source[cell // cx, cell % cx, rows_of[chunk], :], 2 * cell + 1, 1)
            packed = jnp.where(lane // 2 == cell, turned, packed)
        pack[step, rows_of[chunk], :] = packed

    def send_halos(step, chunk):
        for side in range(6):
            @pl.when(exists[side])
            def _(side=side):
                halo_copy(step, chunk, side, False).start()

    def wait_halos(step, chunk):
        for side in range(6):
            @pl.when(exists[side])
            def _(side=side):
                halo_copy(step, chunk, side, True).wait_recv()

    def advance(step, chunk, emit):
        source = (first, second)[step]
        rows = rows_of[chunk]
        above_rows = pl.ds(energies - size * (chunk + 1) + 1, size)
        diffusion, losses, losses_above = coef[0, rows, :], coef[1, rows, :], coef[2, rows, :]
        left = pltpu.roll(halo_y[step, 0, rows, :], 1, 1)
        right = pltpu.roll(halo_y[step, 1, rows, :], lanes - 1, 1)
        faces = jnp.where(lane % 2 == 1, left, right)
        for z in range(cz):
            for x in range(cx):
                cell = z * cx + x
                center = source[z, x, rows, :]
                above = source[z, x, above_rows, :]
                beside = (source[z - 1, x, rows, :] if z else halo_z[step, 0, x, rows, :]) + (
                    source[z + 1, x, rows, :] if z < cz - 1 else halo_z[step, 1, x, rows, :])
                beside = beside + (source[z, x - 1, rows, :] if x else halo_x[step, 0, z, rows, :])
                beside = beside + (
                    source[z, x + 1, rows, :] if x < cx - 1 else halo_x[step, 1, z, rows, :])
                face = pltpu.roll(faces, lanes - (2 * cell + 1), 1)
                beside = beside + jnp.where(lane == 0, face, pltpu.roll(center, 1, 1))
                beside = beside + jnp.where(lane == lanes - 1, face, pltpu.roll(center, lanes - 1, 1))
                new = center + diffusion * (beside - 6.0 * center) + losses_above * above
                emit(z, x, new - losses * center)

    def first_step(chunk):
        def emit(z, x, new):
            second[z, x, rows_of[chunk], :] = new
        advance(0, chunk, emit)
        pack_rows(1, chunk)

    def second_step(chunk):
        start = energies - size * (chunk + 1)

        def emit(z, x, new):
            cell = z * cx + x
            out_ref[pl.ds(start * cells + cell, size, stride=cells), :] = new
            shining = gas_ref[cell:cell + 1, :] * new
            high = shining.astype(jnp.bfloat16)
            low = (shining - high.astype(jnp.float32)).astype(jnp.bfloat16)
            lhs[chunk, 0:size, cell * lanes:(cell + 1) * lanes] = high
            lhs[chunk, size:2 * size, cell * lanes:(cell + 1) * lanes] = low
        advance(1, chunk, emit)

    owners = [owner_ref[s] for s in range(slot_count)]
    blocks = [block_ref[s] for s in range(slot_count)]
    ranks = []
    for s in range(slot_count):
        rank = jnp.int32(0)
        for t in range(s):
            rank = rank + jnp.where(owners[t] == owners[s], 1, 0)
        ranks.append(rank)

    chosen = []
    for offset in range(ny):
        who = lax.rem(gy + offset, ny)
        entry = []
        table = jnp.full((8, lanes), -1.0, jnp.float32)
        place = lax.broadcasted_iota(jnp.int32, (8, lanes), 0)
        for c in range(CAP):
            index, name = jnp.int32(0), jnp.int32(-1)
            for s in range(slot_count):
                hit = jnp.logical_and(owners[s] == who, ranks[s] == c)
                index = jnp.where(hit, s, index)
                name = jnp.where(hit, blocks[s], name)
            entry.append(index)
            table = jnp.where(place == c, name.astype(jnp.float32), table)
        chosen.append(entry)
        names[offset] = table

    def sky_copy(chunk, offset):
        return pltpu.make_async_remote_copy(
            src_ref=slots.at[chunk, offset], dst_ref=landed.at[chunk, offset - 1],
            send_sem=sky_send.at[chunk, offset - 1], recv_sem=sky_recv.at[chunk, offset - 1],
            device_id=(gx, lax.rem(gy + offset, ny), gz), device_id_type=MESH,
        )

    def name_copy(offset):
        return pltpu.make_async_remote_copy(
            src_ref=names.at[offset], dst_ref=landed_names.at[offset - 1],
            send_sem=name_send.at[offset - 1], recv_sem=name_recv.at[offset - 1],
            device_id=(gx, lax.rem(gy + offset, ny), gz), device_id_type=MESH,
        )

    def project(chunk):
        for s in range(0, slot_count, 2):
            pair = [weights[t] for t in range(s, min(s + 2, slot_count))]
            rhs = pair[0] if len(pair) == 1 else jnp.concatenate(pair, axis=1)
            product = jnp.dot(lhs[chunk], rhs, preferred_element_type=jnp.float32)
            product = product[0:size] + product[size:2 * size]
            for t in range(len(pair)):
                contrib[chunk, s + t] = product[:, t * lanes:(t + 1) * lanes]
        for offset in range(1, ny):
            for c in range(CAP):
                slots[chunk, offset, c] = contrib[chunk, chosen[offset][c]]
            sky_copy(chunk, offset).start()

    for chunk in range(CHUNKS):
        pack_rows(0, chunk)

    partners = ny - 1
    for side in range(4):
        partners = partners + jnp.where(exists[side], 1, 0)
    pl.semaphore_wait(barrier, partners)

    send_halos(0, 0)
    if CHUNKS > 1:
        send_halos(0, 1)
    for offset in range(1, ny):
        name_copy(offset).start()
    for chunk in range(CHUNKS + 1):
        if chunk < CHUNKS:
            wait_halos(0, chunk)
            first_step(chunk)
            send_halos(1, chunk)
            if chunk + 2 < CHUNKS:
                send_halos(0, chunk + 2)
        if chunk == 1:
            load.wait()
        if chunk:
            wait_halos(1, chunk - 1)
            second_step(chunk - 1)
            project(chunk - 1)

    for offset in range(1, ny):
        name_copy(offset).wait_recv()
    totals = []
    for chunk in range(CHUNKS):
        total = [jnp.zeros((size, lanes), jnp.float32) for _ in range(BO)]
        for offset in range(ny):
            if offset:
                sky_copy(chunk, offset).wait_recv()
            for c in range(CAP):
                if offset:
                    term = landed[chunk, offset - 1, c]
                    name = landed_names[offset - 1, c:c + 1, :]
                else:
                    term = contrib[chunk, chosen[0][c]]
                    name = names[0, c:c + 1, :]
                for b in range(BO):
                    total[b] = total[b] + jnp.where(name == float(b), term, 0.0)
        totals.append(jnp.concatenate(total, axis=1))
    summed = jnp.concatenate(totals[::-1], axis=0)
    sky = jnp.dot(
        pi0_ref[...], summed, precision=lax.Precision.HIGHEST, preferred_element_type=jnp.float32
    )
    for b in range(BO):
        sky_ref[b] = sky[:, b * lanes:(b + 1) * lanes]

    for step in range(2):
        for chunk in range(CHUNKS):
            for side in range(6):
                @pl.when(exists[side])
                def _(step=step, chunk=chunk, side=side):
                    halo_copy(step, chunk, side, False).wait_send()
    for offset in range(1, ny):
        name_copy(offset).wait_send()
        for chunk in range(CHUNKS):
            sky_copy(chunk, offset).wait_send()


def body(sizes, cr_init, gas, diff_coeff, loss_coeff, pi0_table, los_weight, slot_owner, slot_block):
    energies, cz, cx, cy = cr_init.shape
    gammas = pi0_table.shape[0]
    slot_count, cells, pixels = los_weight.shape[3:]
    ny = sizes[1]
    size = energies // CHUNKS
    f32 = jnp.float32
    vmem = pl.BlockSpec(memory_space=pltpu.VMEM)
    smem = pl.BlockSpec(memory_space=pltpu.SMEM)
    density, sky = pl.pallas_call(
        functools.partial(kernel, sizes),
        out_shape=(
            jax.ShapeDtypeStruct((energies * cz * cx, cy), f32),
            jax.ShapeDtypeStruct((BO, gammas, pixels), f32),
        ),
        in_specs=[vmem] * 5 + [smem] * 2 + [pl.BlockSpec(memory_space=pl.ANY)],
        out_specs=(vmem, vmem),
        scratch_shapes=[
            pltpu.VMEM((cz, cx, energies + PAD, cy), f32),
            pltpu.VMEM((cz, cx, energies + PAD, cy), f32),
            pltpu.VMEM((2, 2, cx, energies, cy), f32),
            pltpu.VMEM((2, 2, cz, energies, cy), f32),
            pltpu.VMEM((2, 2, energies, cy), f32),
            pltpu.VMEM((2, energies, cy), f32),
            pltpu.VMEM((3, energies, cy), f32),
            pltpu.VMEM((slot_count, cells, pixels), los_weight.dtype),
            pltpu.VMEM((CHUNKS, 2 * size, cells), jnp.bfloat16),
            pltpu.VMEM((CHUNKS, slot_count, size, pixels), f32),
            pltpu.VMEM((CHUNKS, ny, CAP, size, pixels), f32),
            pltpu.VMEM((CHUNKS, ny - 1, CAP, size, pixels), f32),
            pltpu.VMEM((ny, 8, pixels), f32),
            pltpu.VMEM((ny - 1, 8, pixels), f32),
            pltpu.SemaphoreType.DMA,
            pltpu.SemaphoreType.DMA((2, CHUNKS, 6)),
            pltpu.SemaphoreType.DMA((2, CHUNKS, 6)),
            pltpu.SemaphoreType.DMA((CHUNKS, ny - 1)),
            pltpu.SemaphoreType.DMA((CHUNKS, ny - 1)),
            pltpu.SemaphoreType.DMA((ny - 1,)),
            pltpu.SemaphoreType.DMA((ny - 1,)),
        ],
        compiler_params=pltpu.CompilerParams(
            collective_id=0, has_side_effects=True, vmem_limit_bytes=48 * 1024 * 1024
        ),
    )(
        cr_init.reshape(energies * cz * cx, cy), gas.reshape(cz * cx, cy),
        diff_coeff.reshape(1, energies), loss_coeff.reshape(1, energies), pi0_table,
        slot_owner.reshape(slot_count), slot_block.reshape(slot_count),
        los_weight.reshape(slot_count, cells, pixels),
    )
    return density.reshape(cr_init.shape), sky.reshape(1, 1, BO, gammas, pixels)


def solution(mesh):
    sizes = (mesh.shape["gx"], mesh.shape["gy"], mesh.shape["gz"])
    in_specs = (
        P(None, "gz", "gx", "gy"),
        P("gz", "gx", "gy"),
        P(),
        P(),
        P(),
        P("gz", "gx", "gy", None, None, None),
        P("gz", "gx", "gy", None, None),
        P("gz", "gx", "gy", None),
    )
    out_specs = (P(None, "gz", "gx", "gy"), P("gz", "gx", "gy", None, None))
    return jax.shard_map(
        functools.partial(body, sizes), mesh=mesh, in_specs=in_specs, out_specs=out_specs,
        check_vma=False,
    )
```

```python
import functools

import jax
import jax.numpy as jnp
from jax import lax
from jax.experimental import pallas as pl
from jax.experimental.pallas import tpu as pltpu
from jax.sharding import PartitionSpec as P

BO = 4
CAP = 3
CHUNKS = 4
PAD = 8
MESH = pl.DeviceIdType.MESH


def kernel(
    sizes, cr_hbm, gas_hbm, diff_hbm, loss_hbm, pi0_hbm, owner_hbm, block_hbm, weight_hbm,
    out_hbm, sky_hbm,
    cr_ref, gas_ref, diff_ref, loss_ref, pi0_ref, owner_ref, block_ref, out_ref, sky_ref,
    load_sem, out_sem, sky_out_sem, first, second, halo_z, halo_x, halo_y, pack, coef, weights, lhs, contrib, slots, landed,
    names, landed_names,
    weight_sem, halo_send, halo_recv, sky_send, sky_recv, name_send, name_recv,
):
    nx, ny, nz = sizes
    energies = diff_hbm.shape[1]
    cz, cx = first.shape[0], first.shape[1]
    lanes = first.shape[3]
    cells = cz * cx
    size = energies // CHUNKS
    slot_count = weights.shape[0]
    gx, gy, gz = lax.axis_index("gx"), lax.axis_index("gy"), lax.axis_index("gz")

    exists = (gz > 0, gz < nz - 1, gx > 0, gx < nx - 1, gy > 0, gy < ny - 1)
    places = (
        (gx, gy, gz - 1), (gx, gy, gz + 1), (gx - 1, gy, gz), (gx + 1, gy, gz),
        (gx, gy - 1, gz), (gx, gy + 1, gz),
    )

    barrier = pltpu.get_barrier_semaphore()
    for side in range(4):
        @pl.when(exists[side])
        def _(side=side):
            pl.semaphore_signal(barrier, inc=1, device_id=places[side], device_id_type=MESH)
    for offset in range(1, ny):
        pl.semaphore_signal(
            barrier, inc=1, device_id=(gx, lax.rem(gy + offset, ny), gz), device_id_type=MESH
        )

    loads = [
        pltpu.make_async_copy(source, target, load_sem.at[index])
        for index, (source, target) in enumerate((
            (cr_hbm, cr_ref), (diff_hbm, diff_ref), (loss_hbm, loss_ref), (gas_hbm, gas_ref),
            (owner_hbm, owner_ref), (block_hbm, block_ref), (pi0_hbm, pi0_ref),
        ))
    ]
    for copy in loads:
        copy.start()
    load = pltpu.make_async_copy(weight_hbm, weights, weight_sem)
    load.start()

    loads[0].wait()
    for cell in range(cells):
        first[cell // cx, cell % cx, 0:energies, :] = cr_ref[pl.ds(cell, energies, stride=cells), :]
    first[:, :, energies:, :] = jnp.zeros((cz, cx, PAD, lanes), jnp.float32)
    second[:, :, energies:, :] = jnp.zeros((cz, cx, PAD, lanes), jnp.float32)

    for copy in loads[1:]:
        copy.wait()
    row = lax.broadcasted_iota(jnp.int32, (energies, energies), 0)
    column = lax.broadcasted_iota(jnp.int32, (energies, energies), 1)
    diff = jnp.broadcast_to(diff_ref[...], (energies, energies))
    loss = jnp.broadcast_to(loss_ref[...], (energies, energies))
    for index, (values, mask) in enumerate(
        ((diff, row == column), (loss, row == column), (loss, row + 1 == column))
    ):
        spread = jnp.sum(jnp.where(mask, values, 0.0), axis=1, keepdims=True)
        coef[index] = jnp.broadcast_to(spread, (energies, lanes))

    for side in range(6):
        @pl.when(jnp.logical_not(exists[side]))
        def _(side=side):
            halo = (halo_z, halo_x, halo_y)[side // 2]
            for step in range(2):
                halo[step, side % 2] = jnp.zeros(halo.shape[2:], jnp.float32)

    lane = lax.broadcasted_iota(jnp.int32, (size, lanes), 1)
    rows_of = [pl.ds(energies - size * (c + 1), size) for c in range(CHUNKS)]

    def halo_copy(step, chunk, side, arriving):
        rows = rows_of[chunk]
        source = (first, second)[step]
        far = side % 2 == 1
        if side < 2:
            src = source.at[cz - 1 if far else 0, :, rows, :]
        elif side < 4:
            src = source.at[:, cx - 1 if far else 0, rows, :]
        else:
            src = pack.at[step, rows, :]
        halo = (halo_z, halo_x, halo_y)[side // 2]
        lands = side % 2 if arriving else 1 - side % 2
        sem_side = side if arriving else side ^ 1
        if side < 4:
            dst = halo.at[step, lands, :, rows, :]
        else:
            dst = halo.at[step, lands, rows, :]
        return pltpu.make_async_remote_copy(
            src_ref=src, dst_ref=dst,
            send_sem=halo_send.at[step, chunk, side],
            recv_sem=halo_recv.at[step, chunk, sem_side],
            device_id=places[side], device_id_type=MESH,
        )

    def pack_rows(step, chunk):
        source = (first, second)[step]
        packed = jnp.zeros((size, lanes), jnp.float32)
        for cell in range(cells):
            turned = pltpu.roll(source[cell // cx, cell % cx, rows_of[chunk], :], 2 * cell + 1, 1)
            packed = jnp.where(lane // 2 == cell, turned, packed)
        pack[step, rows_of[chunk], :] = packed

    def send_halos(step, chunk):
        for side in range(6):
            @pl.when(exists[side])
            def _(side=side):
                halo_copy(step, chunk, side, False).start()

    def wait_halos(step, chunk):
        for side in range(6):
            @pl.when(exists[side])
            def _(side=side):
                halo_copy(step, chunk, side, True).wait_recv()

    def advance(step, chunk, emit):
        source = (first, second)[step]
        rows = rows_of[chunk]
        above_rows = pl.ds(energies - size * (chunk + 1) + 1, size)
        diffusion, losses, losses_above = coef[0, rows, :], coef[1, rows, :], coef[2, rows, :]
        left = pltpu.roll(halo_y[step, 0, rows, :], 1, 1)
        right = pltpu.roll(halo_y[step, 1, rows, :], lanes - 1, 1)
        faces = jnp.where(lane % 2 == 1, left, right)
        for z in range(cz):
            for x in range(cx):
                cell = z * cx + x
                center = source[z, x, rows, :]
                above = source[z, x, above_rows, :]
                beside = (source[z - 1, x, rows, :] if z else halo_z[step, 0, x, rows, :]) + (
                    source[z + 1, x, rows, :] if z < cz - 1 else halo_z[step, 1, x, rows, :])
                beside = beside + (source[z, x - 1, rows, :] if x else halo_x[step, 0, z, rows, :])
                beside = beside + (
                    source[z, x + 1, rows, :] if x < cx - 1 else halo_x[step, 1, z, rows, :])
                face = pltpu.roll(faces, lanes - (2 * cell + 1), 1)
                beside = beside + jnp.where(lane == 0, face, pltpu.roll(center, 1, 1))
                beside = beside + jnp.where(lane == lanes - 1, face, pltpu.roll(center, lanes - 1, 1))
                new = center + diffusion * (beside - 6.0 * center) + losses_above * above
                emit(z, x, new - losses * center)

    def first_step(chunk):
        def emit(z, x, new):
            second[z, x, rows_of[chunk], :] = new
        advance(0, chunk, emit)
        pack_rows(1, chunk)

    def second_step(chunk):
        start = energies - size * (chunk + 1)

        def emit(z, x, new):
            cell = z * cx + x
            out_ref[pl.ds(start * cells + cell, size, stride=cells), :] = new
            shining = gas_ref[cell:cell + 1, :] * new
            high = shining.astype(jnp.bfloat16)
            low = (shining - high.astype(jnp.float32)).astype(jnp.bfloat16)
            lhs[chunk, 0:size, cell * lanes:(cell + 1) * lanes] = high
            lhs[chunk, size:2 * size, cell * lanes:(cell + 1) * lanes] = low
        advance(1, chunk, emit)
        out_copy(chunk).start()

    def out_copy(chunk):
        part = pl.ds((energies - size * (chunk + 1)) * cells, size * cells)
        return pltpu.make_async_copy(out_ref.at[part, :], out_hbm.at[part, :], out_sem.at[chunk])

    owners = [owner_ref[s] for s in range(slot_count)]
    blocks = [block_ref[s] for s in range(slot_count)]
    ranks = []
    for s in range(slot_count):
        rank = jnp.int32(0)
        for t in range(s):
            rank = rank + jnp.where(owners[t] == owners[s], 1, 0)
        ranks.append(rank)

    chosen = []
    for offset in range(ny):
        who = lax.rem(gy + offset, ny)
        entry = []
        table = jnp.full((8, lanes), -1.0, jnp.float32)
        place = lax.broadcasted_iota(jnp.int32, (8, lanes), 0)
        for c in range(CAP):
            index, name = jnp.int32(0), jnp.int32(-1)
            for s in range(slot_count):
                hit = jnp.logical_and(owners[s] == who, ranks[s] == c)
                index = jnp.where(hit, s, index)
                name = jnp.where(hit, blocks[s], name)
            entry.append(index)
            table = jnp.where(place == c, name.astype(jnp.float32), table)
        chosen.append(entry)
        names[offset] = table

    def sky_copy(chunk, offset):
        return pltpu.make_async_remote_copy(
            src_ref=slots.at[chunk, offset], dst_ref=landed.at[chunk, offset - 1],
            send_sem=sky_send.at[chunk, offset - 1], recv_sem=sky_recv.at[chunk, offset - 1],
            device_id=(gx, lax.rem(gy + offset, ny), gz), device_id_type=MESH,
        )

    def name_copy(offset):
        return pltpu.make_async_remote_copy(
            src_ref=names.at[offset], dst_ref=landed_names.at[offset - 1],
            send_sem=name_send.at[offset - 1], recv_sem=name_recv.at[offset - 1],
            device_id=(gx, lax.rem(gy + offset, ny), gz), device_id_type=MESH,
        )

    def project(chunk):
        for s in range(0, slot_count, 2):
            pair = [weights[t] for t in range(s, min(s + 2, slot_count))]
            rhs = pair[0] if len(pair) == 1 else jnp.concatenate(pair, axis=1)
            product = jnp.dot(lhs[chunk], rhs, preferred_element_type=jnp.float32)
            product = product[0:size] + product[size:2 * size]
            for t in range(len(pair)):
                contrib[chunk, s + t] = product[:, t * lanes:(t + 1) * lanes]
        for offset in range(1, ny):
            for c in range(CAP):
                slots[chunk, offset, c] = contrib[chunk, chosen[offset][c]]
            sky_copy(chunk, offset).start()

    for chunk in range(CHUNKS):
        pack_rows(0, chunk)

    partners = ny - 1
    for side in range(4):
        partners = partners + jnp.where(exists[side], 1, 0)
    pl.semaphore_wait(barrier, partners)

    send_halos(0, 0)
    if CHUNKS > 1:
        send_halos(0, 1)
    for offset in range(1, ny):
        name_copy(offset).start()
    for chunk in range(CHUNKS + 1):
        if chunk < CHUNKS:
            wait_halos(0, chunk)
            first_step(chunk)
            send_halos(1, chunk)
            if chunk + 2 < CHUNKS:
                send_halos(0, chunk + 2)
        if chunk == 1:
            load.wait()
        if chunk:
            wait_halos(1, chunk - 1)
            second_step(chunk - 1)
            project(chunk - 1)

    for offset in range(1, ny):
        name_copy(offset).wait_recv()
    totals = []
    for chunk in range(CHUNKS):
        total = [jnp.zeros((size, lanes), jnp.float32) for _ in range(BO)]
        for offset in range(ny):
            if offset:
                sky_copy(chunk, offset).wait_recv()
            for c in range(CAP):
                if offset:
                    term = landed[chunk, offset - 1, c]
                    name = landed_names[offset - 1, c:c + 1, :]
                else:
                    term = contrib[chunk, chosen[0][c]]
                    name = names[0, c:c + 1, :]
                for b in range(BO):
                    total[b] = total[b] + jnp.where(name == float(b), term, 0.0)
        totals.append(jnp.concatenate(total, axis=1))
    summed = jnp.concatenate(totals[::-1], axis=0)
    sky = jnp.dot(
        pi0_ref[...].T, summed, precision=lax.Precision.HIGHEST, preferred_element_type=jnp.float32
    )
    for b in range(BO):
        sky_ref[b] = sky[:, b * lanes:(b + 1) * lanes]
    sky_out = pltpu.make_async_copy(sky_ref, sky_hbm, sky_out_sem)
    sky_out.start()

    for step in range(2):
        for chunk in range(CHUNKS):
            for side in range(6):
                @pl.when(exists[side])
                def _(step=step, chunk=chunk, side=side):
                    halo_copy(step, chunk, side, False).wait_send()
    for offset in range(1, ny):
        name_copy(offset).wait_send()
        for chunk in range(CHUNKS):
            sky_copy(chunk, offset).wait_send()
    for chunk in range(CHUNKS):
        out_copy(chunk).wait()
    sky_out.wait()


def body(sizes, cr_init, gas, diff_coeff, loss_coeff, pi0_table, los_weight, slot_owner, slot_block):
    energies, cz, cx, cy = cr_init.shape
    gammas = pi0_table.shape[0]
    slot_count, cells, pixels = los_weight.shape[3:]
    ny = sizes[1]
    size = energies // CHUNKS
    f32 = jnp.float32
    anywhere = pl.BlockSpec(memory_space=pl.ANY)
    density, sky = pl.pallas_call(
        functools.partial(kernel, sizes),
        out_shape=(
            jax.ShapeDtypeStruct((energies * cz * cx, cy), f32),
            jax.ShapeDtypeStruct((BO, gammas, pixels), f32),
        ),
        in_specs=[anywhere] * 8,
        out_specs=(anywhere, anywhere),
        scratch_shapes=[
            pltpu.VMEM((energies * cz * cx, cy), f32),
            pltpu.VMEM((cz * cx, cy), f32),
            pltpu.VMEM((1, energies), f32),
            pltpu.VMEM((1, energies), f32),
            pltpu.VMEM((energies, gammas), f32),
            pltpu.SMEM((slot_count,), jnp.int32),
            pltpu.SMEM((slot_count,), jnp.int32),
            pltpu.VMEM((energies * cz * cx, cy), f32),
            pltpu.VMEM((BO, gammas, pixels), f32),
            pltpu.SemaphoreType.DMA((7,)),
            pltpu.SemaphoreType.DMA((CHUNKS,)),
            pltpu.SemaphoreType.DMA,
            pltpu.VMEM((cz, cx, energies + PAD, cy), f32),
            pltpu.VMEM((cz, cx, energies + PAD, cy), f32),
            pltpu.VMEM((2, 2, cx, energies, cy), f32),
            pltpu.VMEM((2, 2, cz, energies, cy), f32),
            pltpu.VMEM((2, 2, energies, cy), f32),
            pltpu.VMEM((2, energies, cy), f32),
            pltpu.VMEM((3, energies, cy), f32),
            pltpu.VMEM((slot_count, cells, pixels), los_weight.dtype),
            pltpu.VMEM((CHUNKS, 2 * size, cells), jnp.bfloat16),
            pltpu.VMEM((CHUNKS, slot_count, size, pixels), f32),
            pltpu.VMEM((CHUNKS, ny, CAP, size, pixels), f32),
            pltpu.VMEM((CHUNKS, ny - 1, CAP, size, pixels), f32),
            pltpu.VMEM((ny, 8, pixels), f32),
            pltpu.VMEM((ny - 1, 8, pixels), f32),
            pltpu.SemaphoreType.DMA,
            pltpu.SemaphoreType.DMA((2, CHUNKS, 6)),
            pltpu.SemaphoreType.DMA((2, CHUNKS, 6)),
            pltpu.SemaphoreType.DMA((CHUNKS, ny - 1)),
            pltpu.SemaphoreType.DMA((CHUNKS, ny - 1)),
            pltpu.SemaphoreType.DMA((ny - 1,)),
            pltpu.SemaphoreType.DMA((ny - 1,)),
        ],
        compiler_params=pltpu.CompilerParams(
            collective_id=0, has_side_effects=True, vmem_limit_bytes=63 * 1024 * 1024
        ),
    )(
        cr_init.reshape(energies * cz * cx, cy), gas.reshape(cz * cx, cy),
        diff_coeff.reshape(1, energies), loss_coeff.reshape(1, energies), pi0_table.T,
        slot_owner.reshape(slot_count), slot_block.reshape(slot_count),
        los_weight.reshape(slot_count, cells, pixels),
    )
    return density.reshape(cr_init.shape), sky.reshape(1, 1, BO, gammas, pixels)


def solution(mesh):
    sizes = (mesh.shape["gx"], mesh.shape["gy"], mesh.shape["gz"])
    in_specs = (
        P(None, "gz", "gx", "gy"),
        P("gz", "gx", "gy"),
        P(),
        P(),
        P(),
        P("gz", "gx", "gy", None, None, None),
        P("gz", "gx", "gy", None, None),
        P("gz", "gx", "gy", None),
    )
    out_specs = (P(None, "gz", "gx", "gy"), P("gz", "gx", "gy", None, None))
    return jax.shard_map(
        functools.partial(body, sizes), mesh=mesh, in_specs=in_specs, out_specs=out_specs,
        check_vma=False,
    )
```

```python
import functools

import jax
import jax.numpy as jnp
from jax import lax
from jax.experimental import pallas as pl
from jax.experimental.pallas import tpu as pltpu
from jax.sharding import PartitionSpec as P

BO = 4
CAP = 3
CHUNKS = 4
PAD = 8
MESH = pl.DeviceIdType.MESH


def kernel(
    sizes, cr_hbm, gas_hbm, diff_hbm, loss_hbm, pi0_hbm, owner_hbm, block_hbm, weight_hbm,
    out_hbm, sky_hbm,
    cr_ref, gas_ref, diff_ref, loss_ref, pi0_ref, owner_ref, block_ref, out_ref, sky_ref,
    load_sem, out_sem, sky_out_sem, first, second, halo_z, halo_x, halo_y, pack, coef, weights, lhs, contrib, slots, landed,
    names, landed_names,
    relay, relay_in_send, relay_in_recv, relay_out_send, half_recv,
    weight_sem, halo_send, halo_recv, sky_send, sky_recv, name_send, name_recv,
):
    nx, ny, nz = sizes
    energies = diff_hbm.shape[1]
    cz, cx = first.shape[0], first.shape[1]
    lanes = first.shape[3]
    cells = cz * cx
    size = energies // CHUNKS
    slot_count = weights.shape[0]
    gx, gy, gz = lax.axis_index("gx"), lax.axis_index("gy"), lax.axis_index("gz")

    bent = nx == 2 and nz == 4
    middle = jnp.logical_and(gz > 0, gz < nz - 1)
    real = (gz > 0, gz < nz - 1, gx > 0, gx < nx - 1, gy > 0, gy < ny - 1)
    exists = (gz > 0, gz < nz - 1, gx > 0, gx < nx - 1, gy > 0, gy < ny - 1)
    if bent:
        exists = (
            jnp.logical_and(gz > 0, gz != 2), jnp.logical_and(gz < nz - 1, gz != 1),
        ) + exists[2:]
    places = (
        (gx, gy, gz - 1), (gx, gy, gz + 1), (gx - 1, gy, gz), (gx + 1, gy, gz),
        (gx, gy - 1, gz), (gx, gy + 1, gz),
    )

    barrier = pltpu.get_barrier_semaphore()
    for side in range(4):
        @pl.when(exists[side])
        def _(side=side):
            pl.semaphore_signal(barrier, inc=1, device_id=places[side], device_id_type=MESH)
    if bent:
        pl.semaphore_signal(
            barrier, inc=1, device_id=(gx, gy, lax.rem(gz + 2, nz)), device_id_type=MESH
        )
    for offset in range(1, ny):
        pl.semaphore_signal(
            barrier, inc=1, device_id=(gx, lax.rem(gy + offset, ny), gz), device_id_type=MESH
        )

    loads = [
        pltpu.make_async_copy(source, target, load_sem.at[index])
        for index, (source, target) in enumerate((
            (cr_hbm, cr_ref), (diff_hbm, diff_ref), (loss_hbm, loss_ref), (gas_hbm, gas_ref),
            (owner_hbm, owner_ref), (block_hbm, block_ref), (pi0_hbm, pi0_ref),
        ))
    ]
    for copy in loads:
        copy.start()
    load = pltpu.make_async_copy(weight_hbm, weights, weight_sem)
    load.start()

    loads[0].wait()
    for cell in range(cells):
        first[cell // cx, cell % cx, 0:energies, :] = cr_ref[pl.ds(cell, energies, stride=cells), :]
    first[:, :, energies:, :] = jnp.zeros((cz, cx, PAD, lanes), jnp.float32)
    second[:, :, energies:, :] = jnp.zeros((cz, cx, PAD, lanes), jnp.float32)

    for copy in loads[1:]:
        copy.wait()
    row = lax.broadcasted_iota(jnp.int32, (energies, energies), 0)
    column = lax.broadcasted_iota(jnp.int32, (energies, energies), 1)
    diff = jnp.broadcast_to(diff_ref[...], (energies, energies))
    loss = jnp.broadcast_to(loss_ref[...], (energies, energies))
    for index, (values, mask) in enumerate(
        ((diff, row == column), (loss, row == column), (loss, row + 1 == column))
    ):
        spread = jnp.sum(jnp.where(mask, values, 0.0), axis=1, keepdims=True)
        coef[index] = jnp.broadcast_to(spread, (energies, lanes))

    for side in range(6):
        @pl.when(jnp.logical_not(real[side]))
        def _(side=side):
            halo = (halo_z, halo_x, halo_y)[side // 2]
            for step in range(2):
                halo[step, side % 2] = jnp.zeros(halo.shape[2:], jnp.float32)

    lane = lax.broadcasted_iota(jnp.int32, (size, lanes), 1)
    rows_of = [pl.ds(energies - size * (c + 1), size) for c in range(CHUNKS)]

    def halo_copy(step, chunk, side, arriving):
        rows = rows_of[chunk]
        source = (first, second)[step]
        far = side % 2 == 1
        if side < 2:
            src = source.at[cz - 1 if far else 0, :, rows, :]
        elif side < 4:
            src = source.at[:, cx - 1 if far else 0, rows, :]
        else:
            src = pack.at[step, rows, :]
        halo = (halo_z, halo_x, halo_y)[side // 2]
        lands = side % 2 if arriving else 1 - side % 2
        sem_side = side if arriving else side ^ 1
        if side < 4:
            dst = halo.at[step, lands, :, rows, :]
        else:
            dst = halo.at[step, lands, rows, :]
        return pltpu.make_async_remote_copy(
            src_ref=src, dst_ref=dst,
            send_sem=halo_send.at[step, chunk, side],
            recv_sem=halo_recv.at[step, chunk, sem_side],
            device_id=places[side], device_id_type=MESH,
        )

    half = cx // 2
    way = lax.rem(gz + 1, 2)

    def relay_in(step, chunk, part):
        face = (first, second)[step].at[(cz - 1) * (1 - way)]
        return pltpu.make_async_remote_copy(
            src_ref=face.at[pl.ds(part * half, half), rows_of[chunk], :],
            dst_ref=relay.at[step, way, :, rows_of[chunk], :],
            send_sem=relay_in_send.at[step, chunk, part],
            recv_sem=relay_in_recv.at[step, chunk, way],
            device_id=(gx, gy, part * (nz - 1)), device_id_type=MESH,
        )

    def relay_out(step, chunk, going):
        part = lax.rem(gz, 2)
        return pltpu.make_async_remote_copy(
            src_ref=relay.at[step, going, :, rows_of[chunk], :],
            dst_ref=halo_z.at[step, going, pl.ds(part * half, half), rows_of[chunk], :],
            send_sem=relay_out_send.at[step, chunk, going],
            recv_sem=half_recv.at[step, chunk, part],
            device_id=(gx, gy, 2 - going), device_id_type=MESH,
        )

    def relay_wait(step, chunk, part, going):
        if going is not None:
            place = relay.at[step, going, :, rows_of[chunk], :]
            sem = relay_in_recv.at[step, chunk, going]
        else:
            place = halo_z.at[step, 1 - way, pl.ds(part * half, half), rows_of[chunk], :]
            sem = half_recv.at[step, chunk, part]
        return pltpu.make_async_remote_copy(
            src_ref=place, dst_ref=place, send_sem=relay_in_send.at[step, chunk, 0], recv_sem=sem,
            device_id=(gx, gy, lax.rem(gz + 2, nz)), device_id_type=MESH,
        )

    def pack_rows(step, chunk):
        source = (first, second)[step]
        packed = jnp.zeros((size, lanes), jnp.float32)
        for cell in range(cells):
            turned = pltpu.roll(source[cell // cx, cell % cx, rows_of[chunk], :], 2 * cell + 1, 1)
            packed = jnp.where(lane // 2 == cell, turned, packed)
        pack[step, rows_of[chunk], :] = packed

    def send_halos(step, chunk):
        if bent:
            @pl.when(middle)
            def _():
                for part in range(2):
                    relay_in(step, chunk, part).start()
        for side in range(6):
            @pl.when(exists[side])
            def _(side=side):
                halo_copy(step, chunk, side, False).start()

    def wait_halos(step, chunk):
        if bent:
            @pl.when(jnp.logical_not(middle))
            def _():
                for going in range(2):
                    relay_wait(step, chunk, 0, going).wait_recv()
                    relay_out(step, chunk, going).start()

            @pl.when(middle)
            def _():
                for part in range(2):
                    relay_wait(step, chunk, part, None).wait_recv()
        for side in range(6):
            @pl.when(exists[side])
            def _(side=side):
                halo_copy(step, chunk, side, True).wait_recv()

    def advance(step, chunk, emit):
        source = (first, second)[step]
        rows = rows_of[chunk]
        above_rows = pl.ds(energies - size * (chunk + 1) + 1, size)
        diffusion, losses, losses_above = coef[0, rows, :], coef[1, rows, :], coef[2, rows, :]
        left = pltpu.roll(halo_y[step, 0, rows, :], 1, 1)
        right = pltpu.roll(halo_y[step, 1, rows, :], lanes - 1, 1)
        faces = jnp.where(lane % 2 == 1, left, right)
        for z in range(cz):
            for x in range(cx):
                cell = z * cx + x
                center = source[z, x, rows, :]
                above = source[z, x, above_rows, :]
                beside = (source[z - 1, x, rows, :] if z else halo_z[step, 0, x, rows, :]) + (
                    source[z + 1, x, rows, :] if z < cz - 1 else halo_z[step, 1, x, rows, :])
                beside = beside + (source[z, x - 1, rows, :] if x else halo_x[step, 0, z, rows, :])
                beside = beside + (
                    source[z, x + 1, rows, :] if x < cx - 1 else halo_x[step, 1, z, rows, :])
                face = pltpu.roll(faces, lanes - (2 * cell + 1), 1)
                beside = beside + jnp.where(lane == 0, face, pltpu.roll(center, 1, 1))
                beside = beside + jnp.where(lane == lanes - 1, face, pltpu.roll(center, lanes - 1, 1))
                new = center + diffusion * (beside - 6.0 * center) + losses_above * above
                emit(z, x, new - losses * center)

    def first_step(chunk):
        def emit(z, x, new):
            second[z, x, rows_of[chunk], :] = new
        advance(0, chunk, emit)
        pack_rows(1, chunk)

    def second_step(chunk):
        start = energies - size * (chunk + 1)

        def emit(z, x, new):
            cell = z * cx + x
            out_ref[pl.ds(start * cells + cell, size, stride=cells), :] = new
            shining = gas_ref[cell:cell + 1, :] * new
            high = shining.astype(jnp.bfloat16)
            low = (shining - high.astype(jnp.float32)).astype(jnp.bfloat16)
            lhs[chunk, 0:size, cell * lanes:(cell + 1) * lanes] = high
            lhs[chunk, size:2 * size, cell * lanes:(cell + 1) * lanes] = low
        advance(1, chunk, emit)
        out_copy(chunk).start()

    def out_copy(chunk):
        part = pl.ds((energies - size * (chunk + 1)) * cells, size * cells)
        return pltpu.make_async_copy(out_ref.at[part, :], out_hbm.at[part, :], out_sem.at[chunk])

    owners = [owner_ref[s] for s in range(slot_count)]
    blocks = [block_ref[s] for s in range(slot_count)]
    ranks = []
    for s in range(slot_count):
        rank = jnp.int32(0)
        for t in range(s):
            rank = rank + jnp.where(owners[t] == owners[s], 1, 0)
        ranks.append(rank)

    chosen = []
    for offset in range(ny):
        who = lax.rem(gy + offset, ny)
        entry = []
        table = jnp.full((8, lanes), -1.0, jnp.float32)
        place = lax.broadcasted_iota(jnp.int32, (8, lanes), 0)
        for c in range(CAP):
            index, name = jnp.int32(0), jnp.int32(-1)
            for s in range(slot_count):
                hit = jnp.logical_and(owners[s] == who, ranks[s] == c)
                index = jnp.where(hit, s, index)
                name = jnp.where(hit, blocks[s], name)
            entry.append(index)
            table = jnp.where(place == c, name.astype(jnp.float32), table)
        chosen.append(entry)
        names[offset] = table

    def sky_copy(chunk, offset):
        return pltpu.make_async_remote_copy(
            src_ref=slots.at[chunk, offset], dst_ref=landed.at[chunk, offset - 1],
            send_sem=sky_send.at[chunk, offset - 1], recv_sem=sky_recv.at[chunk, offset - 1],
            device_id=(gx, lax.rem(gy + offset, ny), gz), device_id_type=MESH,
        )

    def name_copy(offset):
        return pltpu.make_async_remote_copy(
            src_ref=names.at[offset], dst_ref=landed_names.at[offset - 1],
            send_sem=name_send.at[offset - 1], recv_sem=name_recv.at[offset - 1],
            device_id=(gx, lax.rem(gy + offset, ny), gz), device_id_type=MESH,
        )

    def project(chunk):
        for s in range(0, slot_count, 2):
            pair = [weights[t] for t in range(s, min(s + 2, slot_count))]
            rhs = pair[0] if len(pair) == 1 else jnp.concatenate(pair, axis=1)
            product = jnp.dot(lhs[chunk], rhs, preferred_element_type=jnp.float32)
            product = product[0:size] + product[size:2 * size]
            for t in range(len(pair)):
                contrib[chunk, s + t] = product[:, t * lanes:(t + 1) * lanes]
        for offset in range(1, ny):
            for c in range(CAP):
                slots[chunk, offset, c] = contrib[chunk, chosen[offset][c]]
            sky_copy(chunk, offset).start()

    for chunk in range(CHUNKS):
        pack_rows(0, chunk)

    partners = ny - 1 + (1 if bent else 0)
    for side in range(4):
        partners = partners + jnp.where(exists[side], 1, 0)
    pl.semaphore_wait(barrier, partners)

    send_halos(0, 0)
    if CHUNKS > 1:
        send_halos(0, 1)
    for offset in range(1, ny):
        name_copy(offset).start()
    for chunk in range(CHUNKS + 1):
        if chunk < CHUNKS:
            wait_halos(0, chunk)
            first_step(chunk)
            send_halos(1, chunk)
            if chunk + 2 < CHUNKS:
                send_halos(0, chunk + 2)
        if chunk == 1:
            load.wait()
        if chunk:
            wait_halos(1, chunk - 1)
            second_step(chunk - 1)
            project(chunk - 1)

    for offset in range(1, ny):
        name_copy(offset).wait_recv()
    totals = []
    for chunk in range(CHUNKS):
        total = [jnp.zeros((size, lanes), jnp.float32) for _ in range(BO)]
        for offset in range(ny):
            if offset:
                sky_copy(chunk, offset).wait_recv()
            for c in range(CAP):
                if offset:
                    term = landed[chunk, offset - 1, c]
                    name = landed_names[offset - 1, c:c + 1, :]
                else:
                    term = contrib[chunk, chosen[0][c]]
                    name = names[0, c:c + 1, :]
                for b in range(BO):
                    total[b] = total[b] + jnp.where(name == float(b), term, 0.0)
        totals.append(jnp.concatenate(total, axis=1))
    summed = jnp.concatenate(totals[::-1], axis=0)
    sky = jnp.dot(
        pi0_ref[...].T, summed, precision=lax.Precision.HIGHEST, preferred_element_type=jnp.float32
    )
    for b in range(BO):
        sky_ref[b] = sky[:, b * lanes:(b + 1) * lanes]
    sky_out = pltpu.make_async_copy(sky_ref, sky_hbm, sky_out_sem)
    sky_out.start()

    for step in range(2):
        for chunk in range(CHUNKS):
            if bent:
                @pl.when(middle)
                def _(step=step, chunk=chunk):
                    for part in range(2):
                        relay_in(step, chunk, part).wait_send()

                @pl.when(jnp.logical_not(middle))
                def _(step=step, chunk=chunk):
                    for going in range(2):
                        relay_out(step, chunk, going).wait_send()
            for side in range(6):
                @pl.when(exists[side])
                def _(step=step, chunk=chunk, side=side):
                    halo_copy(step, chunk, side, False).wait_send()
    for offset in range(1, ny):
        name_copy(offset).wait_send()
        for chunk in range(CHUNKS):
            sky_copy(chunk, offset).wait_send()
    for chunk in range(CHUNKS):
        out_copy(chunk).wait()
    sky_out.wait()


def hand_over(density_in, sky_in, density_out, sky_out, sems):
    rows = density_in.shape[0] // 4
    copies = [
        pltpu.make_async_copy(
            density_in.at[pl.ds(i * rows, rows), :], density_out.at[pl.ds(i * rows, rows), :],
            sems.at[i],
        )
        for i in range(4)
    ]
    copies.append(pltpu.make_async_copy(sky_in, sky_out, sems.at[4]))
    for copy in copies:
        copy.start()
    for copy in copies:
        copy.wait()


def body(sizes, cr_init, gas, diff_coeff, loss_coeff, pi0_table, los_weight, slot_owner, slot_block):
    energies, cz, cx, cy = cr_init.shape
    gammas = pi0_table.shape[0]
    slot_count, cells, pixels = los_weight.shape[3:]
    ny = sizes[1]
    size = energies // CHUNKS
    f32 = jnp.float32
    anywhere = pl.BlockSpec(memory_space=pl.ANY)
    density, sky = pl.pallas_call(
        functools.partial(kernel, sizes),
        out_shape=(
            jax.ShapeDtypeStruct((energies * cz * cx, cy), f32),
            jax.ShapeDtypeStruct((BO, gammas, pixels), f32),
        ),
        in_specs=[anywhere] * 8,
        out_specs=(anywhere, anywhere),
        scratch_shapes=[
            pltpu.VMEM((energies * cz * cx, cy), f32),
            pltpu.VMEM((cz * cx, cy), f32),
            pltpu.VMEM((1, energies), f32),
            pltpu.VMEM((1, energies), f32),
            pltpu.VMEM((energies, gammas), f32),
            pltpu.SMEM((slot_count,), jnp.int32),
            pltpu.SMEM((slot_count,), jnp.int32),
            pltpu.VMEM((energies * cz * cx, cy), f32),
            pltpu.VMEM((BO, gammas, pixels), f32),
            pltpu.SemaphoreType.DMA((7,)),
            pltpu.SemaphoreType.DMA((CHUNKS,)),
            pltpu.SemaphoreType.DMA,
            pltpu.VMEM((cz, cx, energies + PAD, cy), f32),
            pltpu.VMEM((cz, cx, energies + PAD, cy), f32),
            pltpu.VMEM((2, 2, cx, energies, cy), f32),
            pltpu.VMEM((2, 2, cz, energies, cy), f32),
            pltpu.VMEM((2, 2, energies, cy), f32),
            pltpu.VMEM((2, energies, cy), f32),
            pltpu.VMEM((3, energies, cy), f32),
            pltpu.VMEM((slot_count, cells, pixels), los_weight.dtype),
            pltpu.VMEM((CHUNKS, 2 * size, cells), jnp.bfloat16),
            pltpu.VMEM((CHUNKS, slot_count, size, pixels), f32),
            pltpu.VMEM((CHUNKS, ny, CAP, size, pixels), f32),
            pltpu.VMEM((CHUNKS, ny - 1, CAP, size, pixels), f32),
            pltpu.VMEM((ny, 8, pixels), f32),
            pltpu.VMEM((ny - 1, 8, pixels), f32),
            pltpu.VMEM((2, 2, cx // 2, energies, cy), f32),
            pltpu.SemaphoreType.DMA((2, CHUNKS, 2)),
            pltpu.SemaphoreType.DMA((2, CHUNKS, 2)),
            pltpu.SemaphoreType.DMA((2, CHUNKS, 2)),
            pltpu.SemaphoreType.DMA((2, CHUNKS, 2)),
            pltpu.SemaphoreType.DMA,
            pltpu.SemaphoreType.DMA((2, CHUNKS, 6)),
            pltpu.SemaphoreType.DMA((2, CHUNKS, 6)),
            pltpu.SemaphoreType.DMA((CHUNKS, ny - 1)),
            pltpu.SemaphoreType.DMA((CHUNKS, ny - 1)),
            pltpu.SemaphoreType.DMA((ny - 1,)),
            pltpu.SemaphoreType.DMA((ny - 1,)),
        ],
        compiler_params=pltpu.CompilerParams(
            collective_id=0, has_side_effects=True, vmem_limit_bytes=63 * 1024 * 1024
        ),
    )(
        cr_init.reshape(energies * cz * cx, cy), gas.reshape(cz * cx, cy),
        diff_coeff.reshape(1, energies), loss_coeff.reshape(1, energies), pi0_table.T,
        slot_owner.reshape(slot_count), slot_block.reshape(slot_count),
        los_weight.reshape(slot_count, cells, pixels),
    )
    density, sky = pl.pallas_call(
        hand_over,
        out_shape=(
            jax.ShapeDtypeStruct(density.shape, f32), jax.ShapeDtypeStruct(sky.shape, f32),
        ),
        in_specs=[anywhere] * 2,
        out_specs=(anywhere, anywhere),
        scratch_shapes=[pltpu.SemaphoreType.DMA((5,))],
        compiler_params=pltpu.CompilerParams(vmem_limit_bytes=63 * 1024 * 1024),
    )(density, sky)
    return density.reshape(cr_init.shape), sky.reshape(1, 1, BO, gammas, pixels)


def solution(mesh):
    sizes = (mesh.shape["gx"], mesh.shape["gy"], mesh.shape["gz"])
    in_specs = (
        P(None, "gz", "gx", "gy"),
        P("gz", "gx", "gy"),
        P(),
        P(),
        P(),
        P("gz", "gx", "gy", None, None, None),
        P("gz", "gx", "gy", None, None),
        P("gz", "gx", "gy", None),
    )
    out_specs = (P(None, "gz", "gx", "gy"), P("gz", "gx", "gy", None, None))
    return jax.shard_map(
        functools.partial(body, sizes), mesh=mesh, in_specs=in_specs, out_specs=out_specs,
        check_vma=False,
    )
```

```python
import functools

import jax
import jax.numpy as jnp
from jax import lax
from jax.experimental import pallas as pl
from jax.experimental.pallas import tpu as pltpu
from jax.sharding import PartitionSpec as P

BO = 4
CAP = 3
CHUNKS = 2
PAD = 8
MESH = pl.DeviceIdType.MESH


def kernel(
    sizes, cr_hbm, gas_hbm, diff_hbm, loss_hbm, pi0_hbm, owner_hbm, block_hbm, weight_hbm,
    out_hbm, sky_hbm,
    cr_ref, gas_ref, diff_ref, loss_ref, pi0_ref, owner_ref, block_ref, out_ref, sky_ref,
    load_sem, out_sem, sky_out_sem, first, second, halo_z, halo_x, halo_y, pack, coef, weights, lhs, contrib, slots, landed,
    names, landed_names,
    weight_sem, halo_send, halo_recv, sky_send, sky_recv, name_send, name_recv,
):
    nx, ny, nz = sizes
    energies = diff_hbm.shape[1]
    cz, cx = first.shape[0], first.shape[1]
    lanes = first.shape[3]
    cells = cz * cx
    size = energies // CHUNKS
    slot_count = weights.shape[0]
    gx, gy, gz = lax.axis_index("gx"), lax.axis_index("gy"), lax.axis_index("gz")

    exists = (gz > 0, gz < nz - 1, gx > 0, gx < nx - 1, gy > 0, gy < ny - 1)
    places = (
        (gx, gy, gz - 1), (gx, gy, gz + 1), (gx - 1, gy, gz), (gx + 1, gy, gz),
        (gx, gy - 1, gz), (gx, gy + 1, gz),
    )

    barrier = pltpu.get_barrier_semaphore()
    for side in range(4):
        @pl.when(exists[side])
        def _(side=side):
            pl.semaphore_signal(barrier, inc=1, device_id=places[side], device_id_type=MESH)
    for offset in range(1, ny):
        pl.semaphore_signal(
            barrier, inc=1, device_id=(gx, lax.rem(gy + offset, ny), gz), device_id_type=MESH
        )

    loads = [
        pltpu.make_async_copy(source, target, load_sem.at[index])
        for index, (source, target) in enumerate((
            (cr_hbm, cr_ref), (diff_hbm, diff_ref), (loss_hbm, loss_ref), (gas_hbm, gas_ref),
            (owner_hbm, owner_ref), (block_hbm, block_ref), (pi0_hbm, pi0_ref),
        ))
    ]
    for copy in loads:
        copy.start()
    load = pltpu.make_async_copy(weight_hbm, weights, weight_sem)
    load.start()

    loads[0].wait()
    for cell in range(cells):
        first[cell // cx, cell % cx, 0:energies, :] = cr_ref[pl.ds(cell, energies, stride=cells), :]
    first[:, :, energies:, :] = jnp.zeros((cz, cx, PAD, lanes), jnp.float32)
    second[:, :, energies:, :] = jnp.zeros((cz, cx, PAD, lanes), jnp.float32)

    for copy in loads[1:]:
        copy.wait()
    row = lax.broadcasted_iota(jnp.int32, (energies, energies), 0)
    column = lax.broadcasted_iota(jnp.int32, (energies, energies), 1)
    diff = jnp.broadcast_to(diff_ref[...], (energies, energies))
    loss = jnp.broadcast_to(loss_ref[...], (energies, energies))
    for index, (values, mask) in enumerate(
        ((diff, row == column), (loss, row == column), (loss, row + 1 == column))
    ):
        spread = jnp.sum(jnp.where(mask, values, 0.0), axis=1, keepdims=True)
        coef[index] = jnp.broadcast_to(spread, (energies, lanes))

    for side in range(6):
        @pl.when(jnp.logical_not(exists[side]))
        def _(side=side):
            halo = (halo_z, halo_x, halo_y)[side // 2]
            for step in range(2):
                halo[step, side % 2] = jnp.zeros(halo.shape[2:], jnp.float32)

    lane = lax.broadcasted_iota(jnp.int32, (size, lanes), 1)
    rows_of = [pl.ds(energies - size * (c + 1), size) for c in range(CHUNKS)]

    def halo_copy(step, chunk, side, arriving):
        rows = rows_of[chunk]
        source = (first, second)[step]
        far = side % 2 == 1
        if side < 2:
            src = source.at[cz - 1 if far else 0, :, rows, :]
        elif side < 4:
            src = source.at[:, cx - 1 if far else 0, rows, :]
        else:
            src = pack.at[step, rows, :]
        halo = (halo_z, halo_x, halo_y)[side // 2]
        lands = side % 2 if arriving else 1 - side % 2
        sem_side = side if arriving else side ^ 1
        if side < 4:
            dst = halo.at[step, lands, :, rows, :]
        else:
            dst = halo.at[step, lands, rows, :]
        return pltpu.make_async_remote_copy(
            src_ref=src, dst_ref=dst,
            send_sem=halo_send.at[step, chunk, side],
            recv_sem=halo_recv.at[step, chunk, sem_side],
            device_id=places[side], device_id_type=MESH,
        )

    def pack_rows(step, chunk):
        source = (first, second)[step]
        packed = jnp.zeros((size, lanes), jnp.float32)
        for cell in range(cells):
            turned = pltpu.roll(source[cell // cx, cell % cx, rows_of[chunk], :], 2 * cell + 1, 1)
            packed = jnp.where(lane // 2 == cell, turned, packed)
        pack[step, rows_of[chunk], :] = packed

    def send_halos(step, chunk):
        for side in range(6):
            @pl.when(exists[side])
            def _(side=side):
                halo_copy(step, chunk, side, False).start()

    def wait_halos(step, chunk):
        for side in range(6):
            @pl.when(exists[side])
            def _(side=side):
                halo_copy(step, chunk, side, True).wait_recv()

    def advance(step, chunk, emit):
        source = (first, second)[step]
        rows = rows_of[chunk]
        above_rows = pl.ds(energies - size * (chunk + 1) + 1, size)
        diffusion, losses, losses_above = coef[0, rows, :], coef[1, rows, :], coef[2, rows, :]
        left = pltpu.roll(halo_y[step, 0, rows, :], 1, 1)
        right = pltpu.roll(halo_y[step, 1, rows, :], lanes - 1, 1)
        faces = jnp.where(lane % 2 == 1, left, right)
        for z in range(cz):
            for x in range(cx):
                cell = z * cx + x
                center = source[z, x, rows, :]
                above = source[z, x, above_rows, :]
                beside = (source[z - 1, x, rows, :] if z else halo_z[step, 0, x, rows, :]) + (
                    source[z + 1, x, rows, :] if z < cz - 1 else halo_z[step, 1, x, rows, :])
                beside = beside + (source[z, x - 1, rows, :] if x else halo_x[step, 0, z, rows, :])
                beside = beside + (
                    source[z, x + 1, rows, :] if x < cx - 1 else halo_x[step, 1, z, rows, :])
                face = pltpu.roll(faces, lanes - (2 * cell + 1), 1)
                beside = beside + jnp.where(lane == 0, face, pltpu.roll(center, 1, 1))
                beside = beside + jnp.where(lane == lanes - 1, face, pltpu.roll(center, lanes - 1, 1))
                new = center + diffusion * (beside - 6.0 * center) + losses_above * above
                emit(z, x, new - losses * center)

    def first_step(chunk):
        def emit(z, x, new):
            second[z, x, rows_of[chunk], :] = new
        advance(0, chunk, emit)
        pack_rows(1, chunk)

    def second_step(chunk):
        start = energies - size * (chunk + 1)

        def emit(z, x, new):
            cell = z * cx + x
            out_ref[pl.ds(start * cells + cell, size, stride=cells), :] = new
            shining = gas_ref[cell:cell + 1, :] * new
            high = shining.astype(jnp.bfloat16)
            low = (shining - high.astype(jnp.float32)).astype(jnp.bfloat16)
            lhs[chunk, 0:size, cell * lanes:(cell + 1) * lanes] = high
            lhs[chunk, size:2 * size, cell * lanes:(cell + 1) * lanes] = low
        advance(1, chunk, emit)
        out_copy(chunk).start()

    def out_copy(chunk):
        part = pl.ds((energies - size * (chunk + 1)) * cells, size * cells)
        return pltpu.make_async_copy(out_ref.at[part, :], out_hbm.at[part, :], out_sem.at[chunk])

    owners = [owner_ref[s] for s in range(slot_count)]
    blocks = [block_ref[s] for s in range(slot_count)]
    ranks = []
    for s in range(slot_count):
        rank = jnp.int32(0)
        for t in range(s):
            rank = rank + jnp.where(owners[t] == owners[s], 1, 0)
        ranks.append(rank)

    chosen = []
    for offset in range(ny):
        who = lax.rem(gy + offset, ny)
        entry = []
        table = jnp.full((8, lanes), -1.0, jnp.float32)
        place = lax.broadcasted_iota(jnp.int32, (8, lanes), 0)
        for c in range(CAP):
            index, name = jnp.int32(0), jnp.int32(-1)
            for s in range(slot_count):
                hit = jnp.logical_and(owners[s] == who, ranks[s] == c)
                index = jnp.where(hit, s, index)
                name = jnp.where(hit, blocks[s], name)
            entry.append(index)
            table = jnp.where(place == c, name.astype(jnp.float32), table)
        chosen.append(entry)
        names[offset] = table

    def sky_copy(chunk, offset):
        return pltpu.make_async_remote_copy(
            src_ref=slots.at[chunk, offset], dst_ref=landed.at[chunk, offset - 1],
            send_sem=sky_send.at[chunk, offset - 1], recv_sem=sky_recv.at[chunk, offset - 1],
            device_id=(gx, lax.rem(gy + offset, ny), gz), device_id_type=MESH,
        )

    def name_copy(offset):
        return pltpu.make_async_remote_copy(
            src_ref=names.at[offset], dst_ref=landed_names.at[offset - 1],
            send_sem=name_send.at[offset - 1], recv_sem=name_recv.at[offset - 1],
            device_id=(gx, lax.rem(gy + offset, ny), gz), device_id_type=MESH,
        )

    def project(chunk):
        for s in range(0, slot_count, 2):
            pair = [weights[t] for t in range(s, min(s + 2, slot_count))]
            rhs = pair[0] if len(pair) == 1 else jnp.concatenate(pair, axis=1)
            product = jnp.dot(lhs[chunk], rhs, preferred_element_type=jnp.float32)
            product = product[0:size] + product[size:2 * size]
            for t in range(len(pair)):
                contrib[chunk, s + t] = product[:, t * lanes:(t + 1) * lanes]
        for offset in range(1, ny):
            for c in range(CAP):
                slots[chunk, offset, c] = contrib[chunk, chosen[offset][c]]
            sky_copy(chunk, offset).start()

    for chunk in range(CHUNKS):
        pack_rows(0, chunk)

    partners = ny - 1
    for side in range(4):
        partners = partners + jnp.where(exists[side], 1, 0)
    pl.semaphore_wait(barrier, partners)

    send_halos(0, 0)
    if CHUNKS > 1:
        send_halos(0, 1)
    for offset in range(1, ny):
        name_copy(offset).start()
    for chunk in range(CHUNKS + 1):
        if chunk < CHUNKS:
            wait_halos(0, chunk)
            first_step(chunk)
            send_halos(1, chunk)
            if chunk + 2 < CHUNKS:
                send_halos(0, chunk + 2)
        if chunk == 1:
            load.wait()
        if chunk:
            wait_halos(1, chunk - 1)
            second_step(chunk - 1)
            project(chunk - 1)

    for offset in range(1, ny):
        name_copy(offset).wait_recv()
    totals = []
    for chunk in range(CHUNKS):
        total = [jnp.zeros((size, lanes), jnp.float32) for _ in range(BO)]
        for offset in range(ny):
            if offset:
                sky_copy(chunk, offset).wait_recv()
            for c in range(CAP):
                if offset:
                    term = landed[chunk, offset - 1, c]
                    name = landed_names[offset - 1, c:c + 1, :]
                else:
                    term = contrib[chunk, chosen[0][c]]
                    name = names[0, c:c + 1, :]
                for b in range(BO):
                    total[b] = total[b] + jnp.where(name == float(b), term, 0.0)
        totals.append(jnp.concatenate(total, axis=1))
    summed = jnp.concatenate(totals[::-1], axis=0)
    sky = jnp.dot(
        pi0_ref[...].T, summed, precision=lax.Precision.HIGHEST, preferred_element_type=jnp.float32
    )
    for b in range(BO):
        sky_ref[b] = sky[:, b * lanes:(b + 1) * lanes]
    sky_out = pltpu.make_async_copy(sky_ref, sky_hbm, sky_out_sem)
    sky_out.start()

    for step in range(2):
        for chunk in range(CHUNKS):
            for side in range(6):
                @pl.when(exists[side])
                def _(step=step, chunk=chunk, side=side):
                    halo_copy(step, chunk, side, False).wait_send()
    for offset in range(1, ny):
        name_copy(offset).wait_send()
        for chunk in range(CHUNKS):
            sky_copy(chunk, offset).wait_send()
    for chunk in range(CHUNKS):
        out_copy(chunk).wait()
    sky_out.wait()


def hand_over(density_in, sky_in, density_out, sky_out, density, sky, sems):
    parts = sems.shape[1] - 1
    rows = density_in.shape[0] // parts
    bounds = [pl.ds(i * rows, rows) for i in range(parts)]
    arriving = [
        pltpu.make_async_copy(density_in.at[part, :], density.at[part, :], sems.at[0, i])
        for i, part in enumerate(bounds)
    ] + [pltpu.make_async_copy(sky_in, sky, sems.at[0, parts])]
    leaving = [
        pltpu.make_async_copy(density.at[part, :], density_out.at[part, :], sems.at[1, i])
        for i, part in enumerate(bounds)
    ] + [pltpu.make_async_copy(sky, sky_out, sems.at[1, parts])]
    for copy in arriving:
        copy.start()
    for copy, onward in zip(arriving, leaving):
        copy.wait()
        onward.start()
    for copy in leaving:
        copy.wait()


def body(sizes, cr_init, gas, diff_coeff, loss_coeff, pi0_table, los_weight, slot_owner, slot_block):
    energies, cz, cx, cy = cr_init.shape
    gammas = pi0_table.shape[0]
    slot_count, cells, pixels = los_weight.shape[3:]
    ny = sizes[1]
    size = energies // CHUNKS
    f32 = jnp.float32
    anywhere = pl.BlockSpec(memory_space=pl.ANY)
    density, sky = pl.pallas_call(
        functools.partial(kernel, sizes),
        out_shape=(
            jax.ShapeDtypeStruct((energies * cz * cx, cy), f32),
            jax.ShapeDtypeStruct((BO, gammas, pixels), f32),
        ),
        in_specs=[anywhere] * 8,
        out_specs=(anywhere, anywhere),
        scratch_shapes=[
            pltpu.VMEM((energies * cz * cx, cy), f32),
            pltpu.VMEM((cz * cx, cy), f32),
            pltpu.VMEM((1, energies), f32),
            pltpu.VMEM((1, energies), f32),
            pltpu.VMEM((energies, gammas), f32),
            pltpu.SMEM((slot_count,), jnp.int32),
            pltpu.SMEM((slot_count,), jnp.int32),
            pltpu.VMEM((energies * cz * cx, cy), f32),
            pltpu.VMEM((BO, gammas, pixels), f32),
            pltpu.SemaphoreType.DMA((7,)),
            pltpu.SemaphoreType.DMA((CHUNKS,)),
            pltpu.SemaphoreType.DMA,
            pltpu.VMEM((cz, cx, energies + PAD, cy), f32),
            pltpu.VMEM((cz, cx, energies + PAD, cy), f32),
            pltpu.VMEM((2, 2, cx, energies, cy), f32),
            pltpu.VMEM((2, 2, cz, energies, cy), f32),
            pltpu.VMEM((2, 2, energies, cy), f32),
            pltpu.VMEM((2, energies, cy), f32),
            pltpu.VMEM((3, energies, cy), f32),
            pltpu.VMEM((slot_count, cells, pixels), los_weight.dtype),
            pltpu.VMEM((CHUNKS, 2 * size, cells), jnp.bfloat16),
            pltpu.VMEM((CHUNKS, slot_count, size, pixels), f32),
            pltpu.VMEM((CHUNKS, ny, CAP, size, pixels), f32),
            pltpu.VMEM((CHUNKS, ny - 1, CAP, size, pixels), f32),
            pltpu.VMEM((ny, 8, pixels), f32),
            pltpu.VMEM((ny - 1, 8, pixels), f32),
            pltpu.SemaphoreType.DMA,
            pltpu.SemaphoreType.DMA((2, CHUNKS, 6)),
            pltpu.SemaphoreType.DMA((2, CHUNKS, 6)),
            pltpu.SemaphoreType.DMA((CHUNKS, ny - 1)),
            pltpu.SemaphoreType.DMA((CHUNKS, ny - 1)),
            pltpu.SemaphoreType.DMA((ny - 1,)),
            pltpu.SemaphoreType.DMA((ny - 1,)),
        ],
        compiler_params=pltpu.CompilerParams(
            collective_id=0, has_side_effects=True, vmem_limit_bytes=63 * 1024 * 1024
        ),
    )(
        cr_init.reshape(energies * cz * cx, cy), gas.reshape(cz * cx, cy),
        diff_coeff.reshape(1, energies), loss_coeff.reshape(1, energies), pi0_table.T,
        slot_owner.reshape(slot_count), slot_block.reshape(slot_count),
        los_weight.reshape(slot_count, cells, pixels),
    )
    density, sky = pl.pallas_call(
        hand_over,
        out_shape=(
            jax.ShapeDtypeStruct(density.shape, f32), jax.ShapeDtypeStruct(sky.shape, f32),
        ),
        in_specs=[anywhere] * 2,
        out_specs=(anywhere, anywhere),
        scratch_shapes=[
            pltpu.VMEM(density.shape, f32),
            pltpu.VMEM(sky.shape, f32),
            pltpu.SemaphoreType.DMA((2, 5)),
        ],
        compiler_params=pltpu.CompilerParams(vmem_limit_bytes=63 * 1024 * 1024),
    )(density, sky)
    return density.reshape(cr_init.shape), sky.reshape(1, 1, BO, gammas, pixels)


def solution(mesh):
    sizes = (mesh.shape["gx"], mesh.shape["gy"], mesh.shape["gz"])
    in_specs = (
        P(None, "gz", "gx", "gy"),
        P("gz", "gx", "gy"),
        P(),
        P(),
        P(),
        P("gz", "gx", "gy", None, None, None),
        P("gz", "gx", "gy", None, None),
        P("gz", "gx", "gy", None),
    )
    out_specs = (P(None, "gz", "gx", "gy"), P("gz", "gx", "gy", None, None))
    return jax.shard_map(
        functools.partial(body, sizes), mesh=mesh, in_specs=in_specs, out_specs=out_specs,
        check_vma=False,
    )
```

```python
import functools

import jax
import jax.numpy as jnp
from jax import lax
from jax.experimental import pallas as pl
from jax.experimental.pallas import tpu as pltpu
from jax.sharding import PartitionSpec as P

BO = 4
CAP = 3
CHUNKS = 2
PAD = 8
MESH = pl.DeviceIdType.MESH


def kernel(
    sizes, cr_hbm, gas_hbm, diff_hbm, loss_hbm, pi0_hbm, owner_hbm, block_hbm, weight_hbm,
    out_hbm, sky_hbm,
    cr_ref, gas_ref, diff_ref, loss_ref, pi0_ref, owner_ref, block_ref, out_ref, sky_ref,
    load_sem, out_sem, sky_out_sem, first, second, halo_z, halo_x, halo_y, pack, coef, weights, lhs, contrib, slots, landed,
    names, landed_names,
    weight_sem, halo_send, halo_recv, sky_send, sky_recv, name_send, name_recv,
):
    nx, ny, nz = sizes
    energies = diff_hbm.shape[1]
    cz, cx = first.shape[0], first.shape[1]
    lanes = first.shape[3]
    cells = cz * cx
    size = energies // CHUNKS
    slot_count = weights.shape[0]
    gx, gy, gz = lax.axis_index("gx"), lax.axis_index("gy"), lax.axis_index("gz")

    exists = (gz > 0, gz < nz - 1, gx > 0, gx < nx - 1, gy > 0, gy < ny - 1)
    places = (
        (gx, gy, gz - 1), (gx, gy, gz + 1), (gx - 1, gy, gz), (gx + 1, gy, gz),
        (gx, gy - 1, gz), (gx, gy + 1, gz),
    )

    barrier = pltpu.get_barrier_semaphore()
    for side in range(4):
        @pl.when(exists[side])
        def _(side=side):
            pl.semaphore_signal(barrier, inc=1, device_id=places[side], device_id_type=MESH)
    for offset in range(1, ny):
        pl.semaphore_signal(
            barrier, inc=1, device_id=(gx, lax.rem(gy + offset, ny), gz), device_id_type=MESH
        )

    loads = [
        pltpu.make_async_copy(source, target, load_sem.at[index])
        for index, (source, target) in enumerate((
            (cr_hbm, cr_ref), (diff_hbm, diff_ref), (loss_hbm, loss_ref), (gas_hbm, gas_ref),
            (owner_hbm, owner_ref), (block_hbm, block_ref), (pi0_hbm, pi0_ref),
        ))
    ]
    for copy in loads:
        copy.start()
    load = pltpu.make_async_copy(weight_hbm, weights, weight_sem)
    load.start()

    loads[0].wait()
    for cell in range(cells):
        first[cell // cx, cell % cx, 0:energies, :] = cr_ref[pl.ds(cell, energies, stride=cells), :]

    lane = lax.broadcasted_iota(jnp.int32, (size, lanes), 1)
    rows_of = [pl.ds(energies - size * (c + 1), size) for c in range(CHUNKS)]

    def halo_copy(step, chunk, side, arriving):
        rows = rows_of[chunk]
        source = (first, second)[step]
        far = side % 2 == 1
        if side < 2:
            src = source.at[cz - 1 if far else 0, :, rows, :]
        elif side < 4:
            src = source.at[:, cx - 1 if far else 0, rows, :]
        else:
            src = pack.at[step, rows, :]
        halo = (halo_z, halo_x, halo_y)[side // 2]
        lands = side % 2 if arriving else 1 - side % 2
        sem_side = side if arriving else side ^ 1
        if side < 4:
            dst = halo.at[step, lands, :, rows, :]
        else:
            dst = halo.at[step, lands, rows, :]
        return pltpu.make_async_remote_copy(
            src_ref=src, dst_ref=dst,
            send_sem=halo_send.at[step, chunk, side],
            recv_sem=halo_recv.at[step, chunk, sem_side],
            device_id=places[side], device_id_type=MESH,
        )

    def pack_rows(step, chunk):
        source = (first, second)[step]
        packed = jnp.zeros((size, lanes), jnp.float32)
        for cell in range(cells):
            turned = pltpu.roll(source[cell // cx, cell % cx, rows_of[chunk], :], 2 * cell + 1, 1)
            packed = jnp.where(lane // 2 == cell, turned, packed)
        pack[step, rows_of[chunk], :] = packed

    def send_halos(step, chunk, sides):
        for side in sides:
            @pl.when(exists[side])
            def _(side=side):
                halo_copy(step, chunk, side, False).start()

    def wait_halos(step, chunk):
        for side in range(6):
            @pl.when(exists[side])
            def _(side=side):
                halo_copy(step, chunk, side, True).wait_recv()

    def advance(step, chunk, emit, planes):
        source = (first, second)[step]
        rows = rows_of[chunk]
        above_rows = pl.ds(energies - size * (chunk + 1) + 1, size)
        diffusion, losses, losses_above = coef[0, rows, :], coef[1, rows, :], coef[2, rows, :]
        left = pltpu.roll(halo_y[step, 0, rows, :], 1, 1)
        right = pltpu.roll(halo_y[step, 1, rows, :], lanes - 1, 1)
        faces = jnp.where(lane % 2 == 1, left, right)
        for z in planes:
            for x in range(cx):
                cell = z * cx + x
                center = source[z, x, rows, :]
                above = source[z, x, above_rows, :]
                beside = (source[z - 1, x, rows, :] if z else halo_z[step, 0, x, rows, :]) + (
                    source[z + 1, x, rows, :] if z < cz - 1 else halo_z[step, 1, x, rows, :])
                beside = beside + (source[z, x - 1, rows, :] if x else halo_x[step, 0, z, rows, :])
                beside = beside + (
                    source[z, x + 1, rows, :] if x < cx - 1 else halo_x[step, 1, z, rows, :])
                face = pltpu.roll(faces, lanes - (2 * cell + 1), 1)
                beside = beside + jnp.where(lane == 0, face, pltpu.roll(center, 1, 1))
                beside = beside + jnp.where(lane == lanes - 1, face, pltpu.roll(center, lanes - 1, 1))
                new = center + diffusion * (beside - 6.0 * center) + losses_above * above
                emit(z, x, new - losses * center)

    def first_step(chunk):
        def emit(z, x, new):
            second[z, x, rows_of[chunk], :] = new
        advance(0, chunk, emit, sorted({0, cz - 1}))
        send_halos(1, chunk, range(2))
        advance(0, chunk, emit, range(1, cz - 1))
        send_halos(1, chunk, range(2, 4))
        pack_rows(1, chunk)
        send_halos(1, chunk, range(4, 6))

    def second_step(chunk):
        start = energies - size * (chunk + 1)

        def emit(z, x, new):
            cell = z * cx + x
            out_ref[pl.ds(start * cells + cell, size, stride=cells), :] = new
            shining = gas_ref[cell:cell + 1, :] * new
            high = shining.astype(jnp.bfloat16)
            low = (shining - high.astype(jnp.float32)).astype(jnp.bfloat16)
            lhs[chunk, 0:size, cell * lanes:(cell + 1) * lanes] = high
            lhs[chunk, size:2 * size, cell * lanes:(cell + 1) * lanes] = low
        advance(1, chunk, emit, range(cz))
        out_copy(chunk).start()

    def out_copy(chunk):
        part = pl.ds((energies - size * (chunk + 1)) * cells, size * cells)
        return pltpu.make_async_copy(out_ref.at[part, :], out_hbm.at[part, :], out_sem.at[chunk])

    def sky_copy(chunk, offset):
        return pltpu.make_async_remote_copy(
            src_ref=slots.at[chunk, offset], dst_ref=landed.at[chunk, offset - 1],
            send_sem=sky_send.at[chunk, offset - 1], recv_sem=sky_recv.at[chunk, offset - 1],
            device_id=(gx, lax.rem(gy + offset, ny), gz), device_id_type=MESH,
        )

    def name_copy(offset):
        return pltpu.make_async_remote_copy(
            src_ref=names.at[offset], dst_ref=landed_names.at[offset - 1],
            send_sem=name_send.at[offset - 1], recv_sem=name_recv.at[offset - 1],
            device_id=(gx, lax.rem(gy + offset, ny), gz), device_id_type=MESH,
        )

    def project(chunk):
        for s in range(0, slot_count, 2):
            pair = [weights[t] for t in range(s, min(s + 2, slot_count))]
            rhs = pair[0] if len(pair) == 1 else jnp.concatenate(pair, axis=1)
            product = jnp.dot(lhs[chunk], rhs, preferred_element_type=jnp.float32)
            product = product[0:size] + product[size:2 * size]
            for t in range(len(pair)):
                contrib[chunk, s + t] = product[:, t * lanes:(t + 1) * lanes]
        for offset in range(1, ny):
            for c in range(CAP):
                slots[chunk, offset, c] = contrib[chunk, chosen[offset][c]]
            sky_copy(chunk, offset).start()

    partners = ny - 1
    for side in range(4):
        partners = partners + jnp.where(exists[side], 1, 0)
    pl.semaphore_wait(barrier, partners)

    for chunk in range(min(2, CHUNKS)):
        send_halos(0, chunk, range(4))
    for chunk in range(CHUNKS):
        pack_rows(0, chunk)
        if chunk < 2:
            send_halos(0, chunk, range(4, 6))

    for copy in loads[1:]:
        copy.wait()
    row = lax.broadcasted_iota(jnp.int32, (energies, energies), 0)
    column = lax.broadcasted_iota(jnp.int32, (energies, energies), 1)
    diff = jnp.broadcast_to(diff_ref[...], (energies, energies))
    loss = jnp.broadcast_to(loss_ref[...], (energies, energies))
    for index, (values, mask) in enumerate(
        ((diff, row == column), (loss, row == column), (loss, row + 1 == column))
    ):
        spread = jnp.sum(jnp.where(mask, values, 0.0), axis=1, keepdims=True)
        coef[index] = jnp.broadcast_to(spread, (energies, lanes))

    for side in range(6):
        @pl.when(jnp.logical_not(exists[side]))
        def _(side=side):
            halo = (halo_z, halo_x, halo_y)[side // 2]
            for step in range(2):
                halo[step, side % 2] = jnp.zeros(halo.shape[2:], jnp.float32)
    first[:, :, energies:, :] = jnp.zeros((cz, cx, PAD, lanes), jnp.float32)
    second[:, :, energies:, :] = jnp.zeros((cz, cx, PAD, lanes), jnp.float32)

    owners = [owner_ref[s] for s in range(slot_count)]
    blocks = [block_ref[s] for s in range(slot_count)]
    ranks = []
    for s in range(slot_count):
        rank = jnp.int32(0)
        for t in range(s):
            rank = rank + jnp.where(owners[t] == owners[s], 1, 0)
        ranks.append(rank)

    chosen = []
    for offset in range(ny):
        who = lax.rem(gy + offset, ny)
        entry = []
        table = jnp.full((8, lanes), -1.0, jnp.float32)
        place = lax.broadcasted_iota(jnp.int32, (8, lanes), 0)
        for c in range(CAP):
            index, name = jnp.int32(0), jnp.int32(-1)
            for s in range(slot_count):
                hit = jnp.logical_and(owners[s] == who, ranks[s] == c)
                index = jnp.where(hit, s, index)
                name = jnp.where(hit, blocks[s], name)
            entry.append(index)
            table = jnp.where(place == c, name.astype(jnp.float32), table)
        chosen.append(entry)
        names[offset] = table

    for offset in range(1, ny):
        name_copy(offset).start()
    for chunk in range(CHUNKS + 1):
        if chunk < CHUNKS:
            wait_halos(0, chunk)
            first_step(chunk)
            if chunk + 2 < CHUNKS:
                send_halos(0, chunk + 2, range(6))
        if chunk == 1:
            load.wait()
        if chunk:
            wait_halos(1, chunk - 1)
            second_step(chunk - 1)
            project(chunk - 1)

    for offset in range(1, ny):
        name_copy(offset).wait_recv()
    totals = []
    for chunk in range(CHUNKS):
        total = [jnp.zeros((size, lanes), jnp.float32) for _ in range(BO)]
        for offset in range(ny):
            if offset:
                sky_copy(chunk, offset).wait_recv()
            for c in range(CAP):
                if offset:
                    term = landed[chunk, offset - 1, c]
                    name = landed_names[offset - 1, c:c + 1, :]
                else:
                    term = contrib[chunk, chosen[0][c]]
                    name = names[0, c:c + 1, :]
                for b in range(BO):
                    total[b] = total[b] + jnp.where(name == float(b), term, 0.0)
        totals.append(jnp.concatenate(total, axis=1))
    summed = jnp.concatenate(totals[::-1], axis=0)
    sky = jnp.dot(
        pi0_ref[...].T, summed, precision=lax.Precision.HIGHEST, preferred_element_type=jnp.float32
    )
    for b in range(BO):
        sky_ref[b] = sky[:, b * lanes:(b + 1) * lanes]
    sky_out = pltpu.make_async_copy(sky_ref, sky_hbm, sky_out_sem)
    sky_out.start()

    for step in range(2):
        for chunk in range(CHUNKS):
            for side in range(6):
                @pl.when(exists[side])
                def _(step=step, chunk=chunk, side=side):
                    halo_copy(step, chunk, side, False).wait_send()
    for offset in range(1, ny):
        name_copy(offset).wait_send()
        for chunk in range(CHUNKS):
            sky_copy(chunk, offset).wait_send()
    for chunk in range(CHUNKS):
        out_copy(chunk).wait()
    sky_out.wait()


def hand_over(density_in, sky_in, density_out, sky_out, density, sky, sems):
    parts = sems.shape[1] - 1
    rows = density_in.shape[0] // parts
    bounds = [pl.ds(i * rows, rows) for i in range(parts)]
    arriving = [
        pltpu.make_async_copy(density_in.at[part, :], density.at[part, :], sems.at[0, i])
        for i, part in enumerate(bounds)
    ] + [pltpu.make_async_copy(sky_in, sky, sems.at[0, parts])]
    leaving = [
        pltpu.make_async_copy(density.at[part, :], density_out.at[part, :], sems.at[1, i])
        for i, part in enumerate(bounds)
    ] + [pltpu.make_async_copy(sky, sky_out, sems.at[1, parts])]
    for copy in arriving:
        copy.start()
    for copy, onward in zip(arriving, leaving):
        copy.wait()
        onward.start()
    for copy in leaving:
        copy.wait()


def body(sizes, cr_init, gas, diff_coeff, loss_coeff, pi0_table, los_weight, slot_owner, slot_block):
    energies, cz, cx, cy = cr_init.shape
    gammas = pi0_table.shape[0]
    slot_count, cells, pixels = los_weight.shape[3:]
    ny = sizes[1]
    size = energies // CHUNKS
    f32 = jnp.float32
    anywhere = pl.BlockSpec(memory_space=pl.ANY)
    density, sky = pl.pallas_call(
        functools.partial(kernel, sizes),
        out_shape=(
            jax.ShapeDtypeStruct((energies * cz * cx, cy), f32),
            jax.ShapeDtypeStruct((BO, gammas, pixels), f32),
        ),
        in_specs=[anywhere] * 8,
        out_specs=(anywhere, anywhere),
        scratch_shapes=[
            pltpu.VMEM((energies * cz * cx, cy), f32),
            pltpu.VMEM((cz * cx, cy), f32),
            pltpu.VMEM((1, energies), f32),
            pltpu.VMEM((1, energies), f32),
            pltpu.VMEM((energies, gammas), f32),
            pltpu.SMEM((slot_count,), jnp.int32),
            pltpu.SMEM((slot_count,), jnp.int32),
            pltpu.VMEM((energies * cz * cx, cy), f32),
            pltpu.VMEM((BO, gammas, pixels), f32),
            pltpu.SemaphoreType.DMA((7,)),
            pltpu.SemaphoreType.DMA((CHUNKS,)),
            pltpu.SemaphoreType.DMA,
            pltpu.VMEM((cz, cx, energies + PAD, cy), f32),
            pltpu.VMEM((cz, cx, energies + PAD, cy), f32),
            pltpu.VMEM((2, 2, cx, energies, cy), f32),
            pltpu.VMEM((2, 2, cz, energies, cy), f32),
            pltpu.VMEM((2, 2, energies, cy), f32),
            pltpu.VMEM((2, energies, cy), f32),
            pltpu.VMEM((3, energies, cy), f32),
            pltpu.VMEM((slot_count, cells, pixels), los_weight.dtype),
            pltpu.VMEM((CHUNKS, 2 * size, cells), jnp.bfloat16),
            pltpu.VMEM((CHUNKS, slot_count, size, pixels), f32),
            pltpu.VMEM((CHUNKS, ny, CAP, size, pixels), f32),
            pltpu.VMEM((CHUNKS, ny - 1, CAP, size, pixels), f32),
            pltpu.VMEM((ny, 8, pixels), f32),
            pltpu.VMEM((ny - 1, 8, pixels), f32),
            pltpu.SemaphoreType.DMA,
            pltpu.SemaphoreType.DMA((2, CHUNKS, 6)),
            pltpu.SemaphoreType.DMA((2, CHUNKS, 6)),
            pltpu.SemaphoreType.DMA((CHUNKS, ny - 1)),
            pltpu.SemaphoreType.DMA((CHUNKS, ny - 1)),
            pltpu.SemaphoreType.DMA((ny - 1,)),
            pltpu.SemaphoreType.DMA((ny - 1,)),
        ],
        compiler_params=pltpu.CompilerParams(
            collective_id=0, has_side_effects=True, vmem_limit_bytes=63 * 1024 * 1024
        ),
    )(
        cr_init.reshape(energies * cz * cx, cy), gas.reshape(cz * cx, cy),
        diff_coeff.reshape(1, energies), loss_coeff.reshape(1, energies), pi0_table.T,
        slot_owner.reshape(slot_count), slot_block.reshape(slot_count),
        los_weight.reshape(slot_count, cells, pixels),
    )
    density, sky = pl.pallas_call(
        hand_over,
        out_shape=(
            jax.ShapeDtypeStruct(density.shape, f32), jax.ShapeDtypeStruct(sky.shape, f32),
        ),
        in_specs=[anywhere] * 2,
        out_specs=(anywhere, anywhere),
        scratch_shapes=[
            pltpu.VMEM(density.shape, f32),
            pltpu.VMEM(sky.shape, f32),
            pltpu.SemaphoreType.DMA((2, 5)),
        ],
        compiler_params=pltpu.CompilerParams(vmem_limit_bytes=63 * 1024 * 1024),
    )(density, sky)
    return density.reshape(cr_init.shape), sky.reshape(1, 1, BO, gammas, pixels)


def solution(mesh):
    sizes = (mesh.shape["gx"], mesh.shape["gy"], mesh.shape["gz"])
    in_specs = (
        P(None, "gz", "gx", "gy"),
        P("gz", "gx", "gy"),
        P(),
        P(),
        P(),
        P("gz", "gx", "gy", None, None, None),
        P("gz", "gx", "gy", None, None),
        P("gz", "gx", "gy", None),
    )
    out_specs = (P(None, "gz", "gx", "gy"), P("gz", "gx", "gy", None, None))
    return jax.shard_map(
        functools.partial(body, sizes), mesh=mesh, in_specs=in_specs, out_specs=out_specs,
        check_vma=False,
    )
```

```python
import functools

import jax
import jax.numpy as jnp
from jax import lax
from jax.experimental import pallas as pl
from jax.experimental.pallas import tpu as pltpu
from jax.sharding import PartitionSpec as P

BO = 4
CAP = 3
CHUNKS = 1
PAD = 8
MESH = pl.DeviceIdType.MESH


def kernel(
    sizes, cr_hbm, gas_hbm, diff_hbm, loss_hbm, pi0_hbm, owner_hbm, block_hbm, weight_hbm,
    out_hbm, sky_hbm,
    cr_ref, gas_ref, diff_ref, loss_ref, pi0_ref, owner_ref, block_ref, out_ref, sky_ref,
    load_sem, out_sem, sky_out_sem, first, second, halo_z, halo_x, halo_y, pack, coef, weights, lhs, contrib, slots, landed,
    names, landed_names,
    weight_sem, halo_send, halo_recv, sky_send, sky_recv, name_send, name_recv,
):
    nx, ny, nz = sizes
    energies = diff_hbm.shape[1]
    cz, cx = first.shape[0], first.shape[1]
    lanes = first.shape[3]
    cells = cz * cx
    size = energies // CHUNKS
    slot_count = weights.shape[0]
    gx, gy, gz = lax.axis_index("gx"), lax.axis_index("gy"), lax.axis_index("gz")

    exists = (gz > 0, gz < nz - 1, gx > 0, gx < nx - 1, gy > 0, gy < ny - 1)
    places = (
        (gx, gy, gz - 1), (gx, gy, gz + 1), (gx - 1, gy, gz), (gx + 1, gy, gz),
        (gx, gy - 1, gz), (gx, gy + 1, gz),
    )

    barrier = pltpu.get_barrier_semaphore()
    for side in range(4):
        @pl.when(exists[side])
        def _(side=side):
            pl.semaphore_signal(barrier, inc=1, device_id=places[side], device_id_type=MESH)
    for offset in range(1, ny):
        pl.semaphore_signal(
            barrier, inc=1, device_id=(gx, lax.rem(gy + offset, ny), gz), device_id_type=MESH
        )

    loads = [
        pltpu.make_async_copy(source, target, load_sem.at[index])
        for index, (source, target) in enumerate((
            (cr_hbm, cr_ref), (diff_hbm, diff_ref), (loss_hbm, loss_ref), (gas_hbm, gas_ref),
            (owner_hbm, owner_ref), (block_hbm, block_ref), (pi0_hbm, pi0_ref),
        ))
    ]
    for copy in loads:
        copy.start()
    load = pltpu.make_async_copy(weight_hbm, weights, weight_sem)
    load.start()

    loads[0].wait()
    for cell in range(cells):
        first[cell // cx, cell % cx, 0:energies, :] = cr_ref[pl.ds(cell, energies, stride=cells), :]

    lane = lax.broadcasted_iota(jnp.int32, (size, lanes), 1)
    rows_of = [pl.ds(energies - size * (c + 1), size) for c in range(CHUNKS)]

    def halo_copy(step, chunk, side, arriving):
        rows = rows_of[chunk]
        source = (first, second)[step]
        far = side % 2 == 1
        if side < 2:
            src = source.at[cz - 1 if far else 0, :, rows, :]
        elif side < 4:
            src = source.at[:, cx - 1 if far else 0, rows, :]
        else:
            src = pack.at[step, rows, :]
        halo = (halo_z, halo_x, halo_y)[side // 2]
        lands = side % 2 if arriving else 1 - side % 2
        sem_side = side if arriving else side ^ 1
        if side < 4:
            dst = halo.at[step, lands, :, rows, :]
        else:
            dst = halo.at[step, lands, rows, :]
        return pltpu.make_async_remote_copy(
            src_ref=src, dst_ref=dst,
            send_sem=halo_send.at[step, chunk, side],
            recv_sem=halo_recv.at[step, chunk, sem_side],
            device_id=places[side], device_id_type=MESH,
        )

    def pack_rows(step, chunk):
        source = (first, second)[step]
        packed = jnp.zeros((size, lanes), jnp.float32)
        for cell in range(cells):
            turned = pltpu.roll(source[cell // cx, cell % cx, rows_of[chunk], :], 2 * cell + 1, 1)
            packed = jnp.where(lane // 2 == cell, turned, packed)
        pack[step, rows_of[chunk], :] = packed

    def send_halos(step, chunk, sides):
        for side in sides:
            @pl.when(exists[side])
            def _(side=side):
                halo_copy(step, chunk, side, False).start()

    def wait_halos(step, chunk):
        for side in range(6):
            @pl.when(exists[side])
            def _(side=side):
                halo_copy(step, chunk, side, True).wait_recv()

    def advance(step, chunk, emit, planes):
        source = (first, second)[step]
        rows = rows_of[chunk]
        above_rows = pl.ds(energies - size * (chunk + 1) + 1, size)
        diffusion, losses, losses_above = coef[0, rows, :], coef[1, rows, :], coef[2, rows, :]
        left = pltpu.roll(halo_y[step, 0, rows, :], 1, 1)
        right = pltpu.roll(halo_y[step, 1, rows, :], lanes - 1, 1)
        faces = jnp.where(lane % 2 == 1, left, right)
        for z in planes:
            for x in range(cx):
                cell = z * cx + x
                center = source[z, x, rows, :]
                above = source[z, x, above_rows, :]
                beside = (source[z - 1, x, rows, :] if z else halo_z[step, 0, x, rows, :]) + (
                    source[z + 1, x, rows, :] if z < cz - 1 else halo_z[step, 1, x, rows, :])
                beside = beside + (source[z, x - 1, rows, :] if x else halo_x[step, 0, z, rows, :])
                beside = beside + (
                    source[z, x + 1, rows, :] if x < cx - 1 else halo_x[step, 1, z, rows, :])
                face = pltpu.roll(faces, lanes - (2 * cell + 1), 1)
                beside = beside + jnp.where(lane == 0, face, pltpu.roll(center, 1, 1))
                beside = beside + jnp.where(lane == lanes - 1, face, pltpu.roll(center, lanes - 1, 1))
                new = center + diffusion * (beside - 6.0 * center) + losses_above * above
                emit(z, x, new - losses * center)

    def first_step(chunk):
        def emit(z, x, new):
            second[z, x, rows_of[chunk], :] = new
        advance(0, chunk, emit, sorted({0, cz - 1}))
        send_halos(1, chunk, range(2))
        advance(0, chunk, emit, range(1, cz - 1))
        send_halos(1, chunk, range(2, 4))
        pack_rows(1, chunk)
        send_halos(1, chunk, range(4, 6))

    def second_step(chunk):
        start = energies - size * (chunk + 1)

        def emit(z, x, new):
            cell = z * cx + x
            out_ref[pl.ds(start * cells + cell, size, stride=cells), :] = new
            shining = gas_ref[cell:cell + 1, :] * new
            high = shining.astype(jnp.bfloat16)
            low = (shining - high.astype(jnp.float32)).astype(jnp.bfloat16)
            lhs[chunk, 0:size, cell * lanes:(cell + 1) * lanes] = high
            lhs[chunk, size:2 * size, cell * lanes:(cell + 1) * lanes] = low
        advance(1, chunk, emit, range(cz))
        out_copy(chunk).start()

    def out_copy(chunk):
        part = pl.ds((energies - size * (chunk + 1)) * cells, size * cells)
        return pltpu.make_async_copy(out_ref.at[part, :], out_hbm.at[part, :], out_sem.at[chunk])

    def sky_copy(chunk, offset):
        return pltpu.make_async_remote_copy(
            src_ref=slots.at[chunk, offset], dst_ref=landed.at[chunk, offset - 1],
            send_sem=sky_send.at[chunk, offset - 1], recv_sem=sky_recv.at[chunk, offset - 1],
            device_id=(gx, lax.rem(gy + offset, ny), gz), device_id_type=MESH,
        )

    def name_copy(offset):
        return pltpu.make_async_remote_copy(
            src_ref=names.at[offset], dst_ref=landed_names.at[offset - 1],
            send_sem=name_send.at[offset - 1], recv_sem=name_recv.at[offset - 1],
            device_id=(gx, lax.rem(gy + offset, ny), gz), device_id_type=MESH,
        )

    def project(chunk):
        for s in range(0, slot_count, 2):
            pair = [weights[t] for t in range(s, min(s + 2, slot_count))]
            rhs = pair[0] if len(pair) == 1 else jnp.concatenate(pair, axis=1)
            product = jnp.dot(lhs[chunk], rhs, preferred_element_type=jnp.float32)
            product = product[0:size] + product[size:2 * size]
            for t in range(len(pair)):
                contrib[chunk, s + t] = product[:, t * lanes:(t + 1) * lanes]
        for offset in range(1, ny):
            for c in range(CAP):
                slots[chunk, offset, c] = contrib[chunk, chosen[offset][c]]
            sky_copy(chunk, offset).start()

    partners = ny - 1
    for side in range(4):
        partners = partners + jnp.where(exists[side], 1, 0)
    pl.semaphore_wait(barrier, partners)

    for chunk in range(min(2, CHUNKS)):
        send_halos(0, chunk, range(4))
    for chunk in range(CHUNKS):
        pack_rows(0, chunk)
        if chunk < 2:
            send_halos(0, chunk, range(4, 6))

    for copy in loads[1:]:
        copy.wait()
    row = lax.broadcasted_iota(jnp.int32, (energies, energies), 0)
    column = lax.broadcasted_iota(jnp.int32, (energies, energies), 1)
    diff = jnp.broadcast_to(diff_ref[...], (energies, energies))
    loss = jnp.broadcast_to(loss_ref[...], (energies, energies))
    for index, (values, mask) in enumerate(
        ((diff, row == column), (loss, row == column), (loss, row + 1 == column))
    ):
        spread = jnp.sum(jnp.where(mask, values, 0.0), axis=1, keepdims=True)
        coef[index] = jnp.broadcast_to(spread, (energies, lanes))

    for side in range(6):
        @pl.when(jnp.logical_not(exists[side]))
        def _(side=side):
            halo = (halo_z, halo_x, halo_y)[side // 2]
            for step in range(2):
                halo[step, side % 2] = jnp.zeros(halo.shape[2:], jnp.float32)
    first[:, :, energies:, :] = jnp.zeros((cz, cx, PAD, lanes), jnp.float32)
    second[:, :, energies:, :] = jnp.zeros((cz, cx, PAD, lanes), jnp.float32)

    owners = [owner_ref[s] for s in range(slot_count)]
    blocks = [block_ref[s] for s in range(slot_count)]
    ranks = []
    for s in range(slot_count):
        rank = jnp.int32(0)
        for t in range(s):
            rank = rank + jnp.where(owners[t] == owners[s], 1, 0)
        ranks.append(rank)

    chosen = []
    for offset in range(ny):
        who = lax.rem(gy + offset, ny)
        entry = []
        table = jnp.full((8, lanes), -1.0, jnp.float32)
        place = lax.broadcasted_iota(jnp.int32, (8, lanes), 0)
        for c in range(CAP):
            index, name = jnp.int32(0), jnp.int32(-1)
            for s in range(slot_count):
                hit = jnp.logical_and(owners[s] == who, ranks[s] == c)
                index = jnp.where(hit, s, index)
                name = jnp.where(hit, blocks[s], name)
            entry.append(index)
            table = jnp.where(place == c, name.astype(jnp.float32), table)
        chosen.append(entry)
        names[offset] = table

    for offset in range(1, ny):
        name_copy(offset).start()
    for chunk in range(CHUNKS + 1):
        if chunk < CHUNKS:
            wait_halos(0, chunk)
            first_step(chunk)
            if chunk + 2 < CHUNKS:
                send_halos(0, chunk + 2, range(6))
        if chunk == 1:
            load.wait()
        if chunk:
            wait_halos(1, chunk - 1)
            second_step(chunk - 1)
            project(chunk - 1)

    for offset in range(1, ny):
        name_copy(offset).wait_recv()
    totals = []
    for chunk in range(CHUNKS):
        total = [jnp.zeros((size, lanes), jnp.float32) for _ in range(BO)]
        for offset in range(ny):
            if offset:
                sky_copy(chunk, offset).wait_recv()
            for c in range(CAP):
                if offset:
                    term = landed[chunk, offset - 1, c]
                    name = landed_names[offset - 1, c:c + 1, :]
                else:
                    term = contrib[chunk, chosen[0][c]]
                    name = names[0, c:c + 1, :]
                for b in range(BO):
                    total[b] = total[b] + jnp.where(name == float(b), term, 0.0)
        totals.append(jnp.concatenate(total, axis=1))
    summed = jnp.concatenate(totals[::-1], axis=0)
    sky = jnp.dot(
        pi0_ref[...].T, summed, precision=lax.Precision.HIGHEST, preferred_element_type=jnp.float32
    )
    for b in range(BO):
        sky_ref[b] = sky[:, b * lanes:(b + 1) * lanes]
    sky_out = pltpu.make_async_copy(sky_ref, sky_hbm, sky_out_sem)
    sky_out.start()

    for step in range(2):
        for chunk in range(CHUNKS):
            for side in range(6):
                @pl.when(exists[side])
                def _(step=step, chunk=chunk, side=side):
                    halo_copy(step, chunk, side, False).wait_send()
    for offset in range(1, ny):
        name_copy(offset).wait_send()
        for chunk in range(CHUNKS):
            sky_copy(chunk, offset).wait_send()
    for chunk in range(CHUNKS):
        out_copy(chunk).wait()
    sky_out.wait()


def hand_over(density_in, sky_in, density_out, sky_out, density, sky, sems):
    parts = sems.shape[1] - 1
    rows = density_in.shape[0] // parts
    bounds = [pl.ds(i * rows, rows) for i in range(parts)]
    arriving = [
        pltpu.make_async_copy(density_in.at[part, :], density.at[part, :], sems.at[0, i])
        for i, part in enumerate(bounds)
    ] + [pltpu.make_async_copy(sky_in, sky, sems.at[0, parts])]
    leaving = [
        pltpu.make_async_copy(density.at[part, :], density_out.at[part, :], sems.at[1, i])
        for i, part in enumerate(bounds)
    ] + [pltpu.make_async_copy(sky, sky_out, sems.at[1, parts])]
    for copy in arriving:
        copy.start()
    for copy, onward in zip(arriving, leaving):
        copy.wait()
        onward.start()
    for copy in leaving:
        copy.wait()


def body(sizes, cr_init, gas, diff_coeff, loss_coeff, pi0_table, los_weight, slot_owner, slot_block):
    energies, cz, cx, cy = cr_init.shape
    gammas = pi0_table.shape[0]
    slot_count, cells, pixels = los_weight.shape[3:]
    ny = sizes[1]
    size = energies // CHUNKS
    f32 = jnp.float32
    anywhere = pl.BlockSpec(memory_space=pl.ANY)
    density, sky = pl.pallas_call(
        functools.partial(kernel, sizes),
        out_shape=(
            jax.ShapeDtypeStruct((energies * cz * cx, cy), f32),
            jax.ShapeDtypeStruct((BO, gammas, pixels), f32),
        ),
        in_specs=[anywhere] * 8,
        out_specs=(anywhere, anywhere),
        scratch_shapes=[
            pltpu.VMEM((energies * cz * cx, cy), f32),
            pltpu.VMEM((cz * cx, cy), f32),
            pltpu.VMEM((1, energies), f32),
            pltpu.VMEM((1, energies), f32),
            pltpu.VMEM((energies, gammas), f32),
            pltpu.SMEM((slot_count,), jnp.int32),
            pltpu.SMEM((slot_count,), jnp.int32),
            pltpu.VMEM((energies * cz * cx, cy), f32),
            pltpu.VMEM((BO, gammas, pixels), f32),
            pltpu.SemaphoreType.DMA((7,)),
            pltpu.SemaphoreType.DMA((CHUNKS,)),
            pltpu.SemaphoreType.DMA,
            pltpu.VMEM((cz, cx, energies + PAD, cy), f32),
            pltpu.VMEM((cz, cx, energies + PAD, cy), f32),
            pltpu.VMEM((2, 2, cx, energies, cy), f32),
            pltpu.VMEM((2, 2, cz, energies, cy), f32),
            pltpu.VMEM((2, 2, energies, cy), f32),
            pltpu.VMEM((2, energies, cy), f32),
            pltpu.VMEM((3, energies, cy), f32),
            pltpu.VMEM((slot_count, cells, pixels), los_weight.dtype),
            pltpu.VMEM((CHUNKS, 2 * size, cells), jnp.bfloat16),
            pltpu.VMEM((CHUNKS, slot_count, size, pixels), f32),
            pltpu.VMEM((CHUNKS, ny, CAP, size, pixels), f32),
            pltpu.VMEM((CHUNKS, ny - 1, CAP, size, pixels), f32),
            pltpu.VMEM((ny, 8, pixels), f32),
            pltpu.VMEM((ny - 1, 8, pixels), f32),
            pltpu.SemaphoreType.DMA,
            pltpu.SemaphoreType.DMA((2, CHUNKS, 6)),
            pltpu.SemaphoreType.DMA((2, CHUNKS, 6)),
            pltpu.SemaphoreType.DMA((CHUNKS, ny - 1)),
            pltpu.SemaphoreType.DMA((CHUNKS, ny - 1)),
            pltpu.SemaphoreType.DMA((ny - 1,)),
            pltpu.SemaphoreType.DMA((ny - 1,)),
        ],
        compiler_params=pltpu.CompilerParams(
            collective_id=0, has_side_effects=True, vmem_limit_bytes=63 * 1024 * 1024
        ),
    )(
        cr_init.reshape(energies * cz * cx, cy), gas.reshape(cz * cx, cy),
        diff_coeff.reshape(1, energies), loss_coeff.reshape(1, energies), pi0_table.T,
        slot_owner.reshape(slot_count), slot_block.reshape(slot_count),
        los_weight.reshape(slot_count, cells, pixels),
    )
    density, sky = pl.pallas_call(
        hand_over,
        out_shape=(
            jax.ShapeDtypeStruct(density.shape, f32), jax.ShapeDtypeStruct(sky.shape, f32),
        ),
        in_specs=[anywhere] * 2,
        out_specs=(anywhere, anywhere),
        scratch_shapes=[
            pltpu.VMEM(density.shape, f32),
            pltpu.VMEM(sky.shape, f32),
            pltpu.SemaphoreType.DMA((2, 5)),
        ],
        compiler_params=pltpu.CompilerParams(vmem_limit_bytes=63 * 1024 * 1024),
    )(density, sky)
    return density.reshape(cr_init.shape), sky.reshape(1, 1, BO, gammas, pixels)


def solution(mesh):
    sizes = (mesh.shape["gx"], mesh.shape["gy"], mesh.shape["gz"])
    in_specs = (
        P(None, "gz", "gx", "gy"),
        P("gz", "gx", "gy"),
        P(),
        P(),
        P(),
        P("gz", "gx", "gy", None, None, None),
        P("gz", "gx", "gy", None, None),
        P("gz", "gx", "gy", None),
    )
    out_specs = (P(None, "gz", "gx", "gy"), P("gz", "gx", "gy", None, None))
    return jax.shard_map(
        functools.partial(body, sizes), mesh=mesh, in_specs=in_specs, out_specs=out_specs,
        check_vma=False,
    )
```
